512 devices in a mesh: wide: 64 (over z, y), lev: 8 (over x, core).
Axes of the slice: x: 4, y: 8, z: 8, core: 2. Of those that a mesh axis runs over, the one named last changes fastest.
Arguments:
- alpha: bfloat16 [64, 4, 64, 4096], P('wide', None, 'lev'), may hold values from -6 to 6
- ens: bfloat16 [64, 4, 64, 4096], P('wide', None, 'lev'), may hold values from -16 to 16
- htile: bfloat16 [8, 128, 128], replicated, may hold values from -0.1875 to 0.1875
- vloc: float32 [64, 9], replicated, may hold values from 0.1 to 0.55
- pattern: int32 [32, 8], replicated, may hold values from 0 to 31
- region_sizes: int32 [64], replicated, may hold values from 1 to 128, 4096 in all
- owner: int32 [64], replicated, may hold values from 0 to 63, each once
- cotangent: bfloat16 [4, 64, 8192], P(None, 'lev', 'wide'), may hold values from -6 to 6
Outputs:
- increment: bfloat16 [4, 64, 8192], P(None, 'lev', 'wide')
- gradient: bfloat16 [64, 4, 64, 4096], P('wide', None, 'lev')
The draws below stay inside these ranges and needn't reach their ends.
Inputs may be any that keep to these rules, and one draw needn't show every extreme that they name: `region_sizes`: the entries sum to 4096; the largest equals 128. `owner`: each index of wide appears once. `pattern`: entries of a row may repeat.
All inputs are finite; a program needn't handle non-finite values.
Results may differ from the reference program's by a relative error of at most 0.008.
Values may be sent and summed in bfloat16 or wider, within the bound.
A program may use at most 128 MiB of HBM per device.

```python
import math
import jax
import jax.numpy as jnp
import numpy as np
from jax import lax

F = 4
LEV = 64
VREACH = 4
BLK = 128
KB = 8
MEM = 64
COLS = 4096
RMAX = 128
NB = 32
N_WIDE = 64


def set_ends(result, own_key, least, top_value):
    place = [jax.random.randint(jax.random.fold_in(own_key, axis), (), 0, length) for axis, length in enumerate(result.shape)]
    main_axis = result.shape.index(max(result.shape))
    next_to = place[:main_axis] + [(place[main_axis] + 1) % result.shape[main_axis]] + place[main_axis + 1:]
    return result.at[tuple(place)].set(least).at[tuple(next_to)].set(top_value)


def with_spikes(drawn, key, source, target, parts, factor):
    owner, partner = [(jnp.arange(drawn.shape[axis_at]) // (drawn.shape[axis_at] // parts)).reshape([-1 if axis == axis_at else 1 for axis in range(drawn.ndim)]) for axis_at in (source, target)]
    chosen = jax.random.permutation(key, parts)[partner]
    strong = (owner == chosen) | (owner == (partner + parts // 2) % parts)
    return jnp.where(strong, factor * drawn, drawn)


def block_scale(own_key, dims, pieces, least, high):
    def one(dim, blocks):
        heights = jax.random.uniform(jax.random.fold_in(jax.random.fold_in(own_key, 6), dim), (blocks,), jnp.float32, least / len(pieces), high / len(pieces))
        return jnp.repeat(jnp.exp(heights), dims[dim] // blocks).reshape((-1,) + (1,) * (len(dims) - dim - 1))

    loudness = one(*pieces[0])
    for cut in pieces[1:]:
        loudness = loudness * one(*cut)
    return loudness


def profile(count, total, limit, skew):
    weights = [(1 << 20) // math.isqrt(rank ** skew) + 1 for rank in range(2, count + 1)]
    rest, counts = total - limit - (count - 1), [1] * (count - 1)
    while rest > 0:
        free = [i for i in range(count - 1) if counts[i] < limit]
        whole, budget = sum([weights[i] for i in free]), rest
        for i in free:
            addition = min(limit - counts[i], max(1, budget * weights[i] // whole), rest)
            counts[i] = counts[i] + addition
            rest = rest - addition
    return np.array([limit] + counts)


def uneven_parts(key, number_of, total, bound, skew):
    if number_of == 2:
        one = jax.random.randint(key, (), max(1, total - bound), min(bound, total - 1) + 1)
        return jnp.stack([one, total - one])
    tallies = jnp.asarray(profile(number_of, total, bound, skew), jnp.int32)
    twos = (number_of - 1) // 2
    donor, receiver = tallies[1:1 + 2 * twos:2], tallies[2:2 + 2 * twos:2]
    room = jnp.minimum(donor - 1, bound - receiver)
    passed = jax.random.randint(jax.random.fold_in(key, 1), (twos,), 0, 1 << 20) % (room + 1)
    tallies = tallies.at[1:1 + 2 * twos:2].set(donor - passed).at[2:2 + 2 * twos:2].set(receiver + passed)
    return tallies[jax.random.permutation(jax.random.fold_in(key, 2), number_of)]


def centred(stream_key, dims, scale, most, pieces=(), kind=jnp.bfloat16):
    factor_of = block_scale(stream_key, dims, pieces, -0.22, 0.18) if pieces else 1.0
    entries = jax.random.normal(stream_key, dims, jnp.float32) * scale * factor_of
    return jnp.minimum(jnp.maximum(entries, -most), most).astype(kind)


def noise_with(own_key, extent, width, reach, shards, heavy, held_as=jnp.bfloat16):
    result = width * jax.random.normal(own_key, extent, jnp.float32)
    if shards:
        result = result * block_scale(own_key, extent, shards, -0.22, 0.18)
    return jnp.clip(with_spikes(result, jax.random.fold_in(own_key, 3), *heavy), -reach, reach).astype(held_as)


def setup_inputs(seed: int = 0) -> dict:
    key_of = jax.random.split(jax.random.key(seed), 9)
    alpha = centred(key_of[0], (MEM, F, LEV, COLS), 1.0, 6.0, ((0, 64), (2, 8)))
    ens = noise_with(key_of[1], (MEM, F, LEV, COLS), 1.0, 16.0, ((0, 64), (2, 8)), (0, 3, 64, 4.0))
    htile = centred(key_of[2], (KB, BLK, BLK), (KB * BLK) ** -0.5, 0.1875)
    vloc = jnp.clip(jax.random.uniform(key_of[3], (LEV, 2 * VREACH + 1), jnp.float32, 0.1, 0.55), 0.1, 0.55)
    pattern = set_ends(jax.random.randint(key_of[4], (NB, KB), 0, NB), jax.random.fold_in(key_of[4], 1), 0, NB - 1).astype(jnp.int32)
    region_sizes = uneven_parts(key_of[5], N_WIDE, COLS, RMAX, 2).astype(jnp.int32)
    owner = jax.random.permutation(key_of[6], N_WIDE).astype(jnp.int32)
    cotangent = centred(key_of[7], (F, LEV, N_WIDE * RMAX), 1.0, 6.0, ((1, 8), (2, 64)))
    return dict(alpha=alpha, ens=ens, htile=htile, vloc=vloc, pattern=pattern, region_sizes=region_sizes, owner=owner, cotangent=cotangent)


def slot_table(region_sizes, owner):
    region_ends = jnp.cumsum(region_sizes).astype(jnp.int32)
    region_starts = (region_ends - region_sizes).astype(jnp.int32)
    column_ids = jnp.arange(COLS, dtype=jnp.int32)
    region_of = lax.optimization_barrier(jnp.sum((region_ends[None, :] <= column_ids[:, None]).astype(jnp.int32), axis=1))
    return (owner[region_of] * RMAX + column_ids - region_starts[region_of]).astype(jnp.int32)

def spread(values, pattern, htile):
    flat_rows = values.reshape(F * LEV, NB, BLK)
    summed = jnp.zeros((F * LEV * NB, BLK), jnp.float32)
    for k in range(KB):
        picked = jnp.take(flat_rows, pattern[:, k], axis=1).reshape(F * LEV * NB, BLK)
        summed = summed + jnp.dot(picked, htile[k], preferred_element_type=jnp.float32)
    return summed.reshape(F, LEV, COLS).astype(jnp.bfloat16)

def gather_back(values, pattern, htile):
    moved = jnp.moveaxis(values.reshape(F * LEV, NB, BLK).astype(jnp.float32), 1, 0)
    summed = jnp.zeros((F * LEV * NB, BLK), jnp.float32)
    for k in range(KB):
        selected = jax.ops.segment_sum(moved, pattern[:, k], num_segments=NB).astype(jnp.bfloat16)
        selected = jnp.moveaxis(selected, 0, 1).reshape(F * LEV * NB, BLK)
        summed = summed + jnp.dot(selected, htile[k].T, preferred_element_type=jnp.float32)
    return summed.reshape(F, LEV, COLS).astype(jnp.bfloat16)

def vertical(values, vloc):
    padded = jnp.pad(values.astype(jnp.float32), ((0, 0), (VREACH, VREACH), (0, 0)))
    summed = jnp.zeros(values.shape, jnp.float32)
    for offset in range(-VREACH, VREACH + 1):
        weight = vloc[:, offset + VREACH]
        summed = summed + weight[None, :, None] * padded[:, VREACH + offset:VREACH + offset + LEV, :]
    return summed.astype(jnp.bfloat16)

def vertical_adjoint(values, vloc):
    padded = jnp.pad(values.astype(jnp.float32), ((0, 0), (VREACH, VREACH), (0, 0)))
    vpadded = jnp.pad(vloc, ((VREACH, VREACH), (0, 0)))
    summed = jnp.zeros(values.shape, jnp.float32)
    for offset in range(-VREACH, VREACH + 1):
        weight = vpadded[VREACH - offset:VREACH - offset + LEV, offset + VREACH]
        summed = summed + weight[None, :, None] * padded[:, VREACH - offset:VREACH - offset + LEV, :]
    return summed.astype(jnp.bfloat16)

def reference(alpha, ens, htile, vloc, pattern, region_sizes, owner, cotangent):
    slot_of = slot_table(region_sizes, owner)

    def forward(running, member_pair):
        alpha_one, ens_one = member_pair
        localized = vertical(spread(alpha_one, pattern, htile), vloc)
        return (running + ens_one.astype(jnp.float32) * localized.astype(jnp.float32), None)
    summed, _ = lax.scan(forward, jnp.zeros((F, LEV, COLS), jnp.float32), (alpha, ens))
    column_sum = summed * (1.0 / math.sqrt(MEM))
    increment = jnp.zeros((F, LEV, N_WIDE * RMAX), jnp.float32).at[:, :, slot_of].set(column_sum)
    increment = increment.astype(jnp.bfloat16)
    cot_cols = cotangent[:, :, slot_of]

    def backward(ens_one):
        scaled = (ens_one.astype(jnp.float32) * cot_cols.astype(jnp.float32)).astype(jnp.bfloat16)
        adjoint_mix = vertical_adjoint(scaled, vloc)
        return gather_back(adjoint_mix, pattern, htile)
    gradient = lax.map(backward, ens)
    return (increment, gradient)
```

```python
import functools
import math

import jax
import jax.numpy as jnp
from jax import lax
from jax.experimental import pallas as pl
from jax.experimental.pallas import tpu as pltpu
from jax.sharding import PartitionSpec as P

REACH = 4
MESH = pl.DeviceIdType.MESH
F32 = jnp.float32
BF16 = jnp.bfloat16
I32 = jnp.int32
VMEM_LIMIT = 60 * 1024 * 1024


def iota(shape, dim):
    return lax.broadcasted_iota(I32, shape, dim)


def halves_of(fields):
    first = iota(fields[0].shape, 0) < 4
    low, high = [], []
    for a, b in (fields[0:2], fields[2:4]):
        low.append(jnp.where(first, a, pltpu.roll(b, 4, 0)))
        high.append(jnp.where(first, pltpu.roll(a, 4, 0), b))
    return jnp.concatenate(low + high, axis=0)


def fields_of(rows):
    fields = []
    for pair in range(2):
        low = rows[8 * pair : 8 * pair + 8]
        high = rows[16 + 8 * pair : 24 + 8 * pair]
        first = iota(low.shape, 0) < 4
        fields.append(jnp.where(first, low, pltpu.roll(high, 4, 0)))
        fields.append(jnp.where(first, pltpu.roll(low, 4, 0), high))
    return fields


def kernel(
    side, n_lev, blocks, slots, members, width,
    alpha_h, ens_h, htile_h, vloc_h, pattern_h, sizes_h, owner_h, cot_h,
    inc_h, grad_h,
    alpha_v, ens_v, tile_v, vloc_v, pat_v, size_v, own_v, cot_v, tab_v, tab_s,
    a3, x, tiles_nt, band_v, ens_f, e1, e2, p3, h0, h1, r0, r1, q0, q1, q0f, q1f, t0, t1,
    g0, g1, snap, mixed, run, grad_v, inc_v,
    local_sem, out_sem, ag1_s, ag1_r, ag2_s, ag2_r, rs1_s, rs1_r, rs2_s, rs2_r, up_s, up_r, dn_s, dn_r,
    bup_s, bup_r, bdn_s, bdn_r,
):
    n_wide = side * side
    w_me, l_me = lax.axis_index("wide"), lax.axis_index("lev")
    z_me, y_me = w_me // side, w_me % side
    upper, lower = lax.rem(l_me + 1, n_lev), lax.rem(l_me + n_lev - 1, n_lev)
    steps = range(1, side)

    def along_y(d):
        return lax.rem(y_me + d, side)

    def along_z(d):
        return lax.rem(z_me + d, side)

    def at_y(y):
        return (z_me * side + y, l_me)

    def at_z(z):
        return (z * side + y_me, l_me)

    def remote(src, dst, s, r, device):
        return pltpu.make_async_remote_copy(
            src_ref=src, dst_ref=dst, send_sem=s, recv_sem=r, device_id=device, device_id_type=MESH
        )

    with jax.named_scope("load_and_greet"):
        loads = [
            pltpu.make_async_copy(src, dst, local_sem.at[i])
            for i, (src, dst) in enumerate(
                (
                    (sizes_h, size_v), (owner_h, own_v), (pattern_h, pat_v), (cot_h, cot_v),
                    (alpha_h, alpha_v), (htile_h, tile_v), (vloc_h, vloc_v), (ens_h, ens_v),
                )
            )
        ]
        for load in loads:
            load.start()
        barrier = pltpu.get_barrier_semaphore()
        friends = [at_y(along_y(d)) for d in steps] + [at_z(along_z(d)) for d in steps]
        friends += [(w_me, upper), (w_me, lower)]
        for friend in friends:
            pl.semaphore_signal(barrier, inc=1, device_id=friend, device_id_type=MESH)

    with jax.named_scope("tables"):
        for load in loads[:4]:
            load.wait()
        square = (n_wide, n_wide)
        rows, cols = iota(square, 0), iota(square, 1)
        size_b = jnp.broadcast_to(size_v[...], square)
        own_b = jnp.broadcast_to(own_v[...], square)
        start_c = jnp.sum(jnp.where(cols < rows, size_b, 0), axis=1, keepdims=True)
        size_c = jnp.sum(jnp.where(cols == rows, size_b, 0), axis=1, keepdims=True)
        own_c = jnp.sum(jnp.where(cols == rows, own_b, 0), axis=1, keepdims=True)
        held = own_c == cols
        base = 3 * slots
        tab_v[base : base + 1, 0:n_wide] = jnp.sum(jnp.where(held, start_c, 0), axis=0, keepdims=True)
        tab_v[base + 1 : base + 2, 0:n_wide] = jnp.sum(jnp.where(held, size_c, 0), axis=0, keepdims=True)
        tab_v[base + 2 : base + 3, 0:n_wide] = jnp.sum(jnp.where(cols == rows, start_c, 0), axis=0, keepdims=True)
        tab_v[base + 3 : base + 4, 0:n_wide] = size_v[...]
        tab_v[base + 4 : base + 5, 0:n_wide] = own_v[...]
        ends = iota((n_wide, blocks), 1) * 128 + 127
        covered = jnp.sum(jnp.where(start_c + size_c <= ends, 1, 0), axis=0, keepdims=True)
        tab_v[base + 5 : base + 6, 0:blocks] = jnp.minimum(covered, n_wide - 1)
        here, there = iota((blocks, blocks), 0), iota((blocks, blocks), 1)
        for k in range(slots):
            row = pat_v[k : k + 1, :]
            col = jnp.sum(jnp.where(here == there, row, 0), axis=1, keepdims=True)
            tab_v[k : k + 1, 0:blocks] = row
            before = jnp.max(jnp.where((col == row) & (here < there), here, -1), axis=0, keepdims=True)
            tab_v[slots + k : slots + k + 1, 0:blocks] = jnp.where(before < 0, blocks, before)
            last = jnp.max(jnp.where(col == there, here, -1), axis=0, keepdims=True)
            tab_v[2 * slots + k : 2 * slots + k + 1, 0:blocks] = jnp.where(last < 0, blocks, last)
        to_s = pltpu.make_async_copy(tab_v, tab_s, local_sem.at[8])
        to_s.start()
        to_s.wait()
        my_start = tab_s[base, w_me]
        my_size = tab_s[base + 1, w_me]
        my_off = my_start & 127

    lane16 = iota((16, 128), 1)
    lane32 = iota((32, 128), 1)

    with jax.named_scope("cotangent_stage_1"):
        cot = cot_v[...].astype(F32)
        tile = pltpu.roll(halves_of([cot[f] for f in range(4)]), my_off, 1)
        g0[w_me] = tile[:16].astype(BF16)
        g1[y_me * side + z_me] = tile[16:].astype(BF16)
        pl.semaphore_wait(barrier, len(friends))
        i0, i1 = w_me, y_me * side + z_me
        ag1 = []
        for d in steps:
            ag1.append(remote(g0.at[i0], g0.at[i0], ag1_s.at[0, d - 1], ag1_r.at[0, d - 1], at_y(along_y(d))))
            ag1.append(remote(g1.at[i1], g1.at[i1], ag1_s.at[1, d - 1], ag1_r.at[1, d - 1], at_z(along_z(d))))
        for copy in ag1:
            copy.start()

    def block_lanes(b):
        return pl.ds(pl.multiple_of(b * 128, 128), 128)

    with jax.named_scope("spread"):
        loads[4].wait()

        def split_alpha(b, _):
            a = alpha_v[0, :, :, block_lanes(b)].astype(F32)
            a3[b] = halves_of([a[f] for f in range(4)]).astype(BF16)
            return 0

        lax.fori_loop(0, blocks, split_alpha, 0, unroll=4)
        loads[5].wait()
        stacked = tile_v[...].reshape(slots * 128, 128)
        group = min(8, blocks)
        n_groups = blocks // group
        halo1 = []
        ag2 = []
        for c in range(n_groups):

            def pick(i, _, c=c):
                b = c * group + i
                at = pl.ds(pl.multiple_of(b * 32, 32), 32)
                for k in range(slots):
                    x[at, k * 128 : (k + 1) * 128] = a3[tab_s[k, b]]
                return 0

            lax.fori_loop(0, group, pick, 0, unroll=2)
            part = jnp.dot(
                x[c * group * 32 : (c + 1) * group * 32, :], stacked, preferred_element_type=F32
            ).astype(BF16)
            for i in range(group):
                b = c * group + i
                e1[0:32, b * 128 : (b + 1) * 128] = part[i * 32 : (i + 1) * 32]
            at = pl.ds(c * group * 128, group * 128)
            sends = [
                remote(e1.at[0:16, at], e1.at[48:64, at], dn_s.at[c], dn_r.at[c], (w_me, lower)),
                remote(e1.at[16:32, at], e1.at[32:48, at], up_s.at[c], up_r.at[c], (w_me, upper)),
            ]
            for copy in sends:
                copy.start()
            halo1 += sends
            if c == 0:
                with jax.named_scope("cotangent_stage_2"):
                    for copy in ag1:
                        copy.wait_recv()
                    at0 = pl.ds(pl.multiple_of(z_me * side, side), side)
                    at1 = pl.ds(pl.multiple_of(y_me * side, side), side)
                    for d in steps:
                        ag2.append(
                            remote(g0.at[at0], g0.at[at0], ag2_s.at[0, d - 1], ag2_r.at[0, d - 1], at_z(along_z(d)))
                        )
                        ag2.append(
                            remote(g1.at[at1], g1.at[at1], ag2_s.at[1, d - 1], ag2_r.at[1, d - 1], at_y(along_y(d)))
                        )
                    for copy in ag2:
                        copy.start()

    with jax.named_scope("bands"):
        loads[6].wait()
        first_level = l_me * 8
        top = n_lev * 8
        half = iota((8, width), 0) < 4

        def pairs_of(v):
            r = pltpu.roll(v, 4, 0)
            return jnp.where(half, v, r), jnp.where(half, r, v)

        band_v[...] = jnp.transpose(vloc_v[...])
        lows, highs = pairs_of(band_v[pl.ds(pl.multiple_of(first_level, 8), 8), :])
        _, before = pairs_of(band_v[pl.ds(pl.multiple_of(jnp.maximum(first_level - 8, 0), 8), 8), :])
        after, _ = pairs_of(band_v[pl.ds(pl.multiple_of(jnp.minimum(first_level + 8, top - 8), 8), 8), :])

        def source_level(k):
            g, q = k // 16, k % 4
            return jnp.where(g == 0, q, jnp.where(g == 1, q + 4, jnp.where(g == 2, q - 4, q + 8)))

        def banded(values, inside, offset):
            total = jnp.zeros(offset.shape, F32)
            for o in range(width):
                column = jnp.broadcast_to(values[:, o : o + 1], offset.shape)
                total = total + jnp.where(inside & (offset == o), column, 0.0)
            return total

        def in_two(w):
            top_part = w.astype(BF16)
            rest = (w - top_part.astype(F32)).astype(BF16)
            return jnp.concatenate([top_part, rest], axis=0)

        shape = (32, 64)
        r, k = iota(shape, 0), iota(shape, 1)
        level_out, level_in = (r // 16) * 4 + r % 4, source_level(k)
        inside = ((r % 16) // 4 == (k % 16) // 4) & (first_level + level_in >= 0) & (first_level + level_in < top)
        down = in_two(
            banded(jnp.concatenate([lows, lows, highs, highs], axis=0), inside, level_in - level_out + REACH)
        )
        shape = (128, 128)
        k, r = iota(shape, 0), iota(shape, 1)
        level_out, level_in = r % 8, source_level(k)
        inside = (r // 8 == (k % 16) // 4) & (first_level + level_in >= 0) & (first_level + level_in < top)
        inside = inside & (k < 64) & (r < 32)
        rows_in = [lows, lows, highs, highs, before, before, after, after] + [jnp.zeros((8, width), F32)] * 8
        up = banded(jnp.concatenate(rows_in, axis=0), inside, level_out - level_in + REACH)
        up = in_two(jnp.transpose(up)[0:32, 0:64])

    with jax.named_scope("ensemble"):
        loads[7].wait()

        def split_ens(b, _):
            a = ens_v[0, :, :, block_lanes(b)].astype(F32)
            ens_f[b] = halves_of([a[f] for f in range(4)])
            return 0

        lax.fori_loop(0, blocks, split_ens, 0, unroll=4)
        for k in range(slots):
            tiles_nt[:, k * 128 : (k + 1) * 128] = tile_v[k]

    with jax.named_scope("mix_down"):
        for copy in halo1:
            copy.wait_recv()
        wide_mix = min(4, blocks)

        def down_step(i, _):
            at = pl.ds(pl.multiple_of(i * wide_mix * 128, wide_mix * 128), wide_mix * 128)
            both = jnp.dot(down, e1[:, at], preferred_element_type=F32)
            local = (both[:32] + both[32:]).astype(BF16).astype(F32)
            for j in range(wide_mix):
                b = i * wide_mix + j
                p3[b] = local[:, j * 128 : (j + 1) * 128] * ens_f[b]
            return 0

        lax.fori_loop(0, blocks // wide_mix, down_step, 0, unroll=2)

    with jax.named_scope("member_sum_stage_1"):

        def share(w, _):
            start = tab_s[base, w]
            blk = lax.shift_right_logical(start, 7)
            t = jnp.where(lane32 >= (start & 127), p3[blk], p3[jnp.minimum(blk + 1, blocks - 1)]).astype(BF16)
            h0[w] = t[:16]
            h1[lax.rem(w, side) * side + lax.div(w, side)] = t[16:]
            return 0

        lax.fori_loop(0, n_wide, share, 0, unroll=4)
        rs1 = []
        for d in steps:
            z, y = along_z(d), along_y(d)
            at0 = pl.ds(pl.multiple_of(z * side, side), side)
            at1 = pl.ds(pl.multiple_of(y * side, side), side)
            rs1.append(remote(h0.at[at0], r0.at[d - 1], rs1_s.at[0, d - 1], rs1_r.at[0, d - 1], at_z(z)))
            rs1.append(remote(h1.at[at1], r1.at[d - 1], rs1_s.at[1, d - 1], rs1_r.at[1, d - 1], at_y(y)))
        for copy in rs1:
            copy.start()

    with jax.named_scope("scaled"):
        for copy in ag2:
            copy.wait_recv()

        def paint(r, acc):
            o = tab_s[base + 4, r]
            start, size = tab_s[base + 2, r] & 127, tab_s[base + 3, r]
            tile = jnp.concatenate([g0[o], g1[(o & (side - 1)) * side + lax.div(o, side)]], axis=0).astype(F32)
            acc = jnp.where((lane32 >= start) & (lane32 < start + size), tile, acc)
            snap[r] = acc
            return jnp.where(lane32 < start + size - 128, tile, acc)

        lax.fori_loop(0, n_wide, paint, jnp.zeros((32, 128), F32), unroll=4)
        halo2 = []
        for c in range(n_groups):

            def scale(i, _, c=c):
                b = c * group + i
                e2[0:32, block_lanes(b)] = (ens_f[b] * snap[tab_s[base + 5, b]]).astype(BF16)
                return 0

            lax.fori_loop(0, group, scale, 0, unroll=4)
            at = pl.ds(c * group * 128, group * 128)
            sends = [
                remote(e2.at[0:16, at], e2.at[48:64, at], bdn_s.at[c], bdn_r.at[c], (w_me, lower)),
                remote(e2.at[16:32, at], e2.at[32:48, at], bup_s.at[c], bup_r.at[c], (w_me, upper)),
            ]
            for copy in sends:
                copy.start()
            halo2 += sends

    with jax.named_scope("mix_up"):
        for k in range(slots):
            run[k, blocks] = jnp.zeros((32, 128), F32)
        for copy in halo2:
            copy.wait_recv()

        def up_step(i, _):
            at = pl.ds(pl.multiple_of(i * wide_mix * 128, wide_mix * 128), wide_mix * 128)
            both = jnp.dot(up, e2[:, at], preferred_element_type=F32)
            local = (both[:32] + both[32:]).astype(BF16).astype(F32)
            for j in range(wide_mix):
                mixed[i * wide_mix + j] = local[:, j * 128 : (j + 1) * 128]
            return 0

        lax.fori_loop(0, blocks // wide_mix, up_step, 0, unroll=2)

        def link(b, _):
            m = mixed[b]
            for k in range(slots):
                run[k, b] = m + run[k, tab_s[slots + k, b]]
            return 0

        lax.fori_loop(0, blocks, link, 0)

    with jax.named_scope("gradient"):
        outs = []
        for c in range(n_groups):

            def pick_back(i, _, c=c):
                j = c * group + i
                at = pl.ds(pl.multiple_of(j * 32, 32), 32)
                for k in range(slots):
                    x[at, k * 128 : (k + 1) * 128] = run[k, tab_s[2 * slots + k, j]].astype(BF16)
                return 0

            lax.fori_loop(0, group, pick_back, 0, unroll=2)
            part = lax.dot_general(
                x[c * group * 32 : (c + 1) * group * 32, :],
                tiles_nt[...],
                (((1,), (1,)), ((), ())),
                preferred_element_type=F32,
            )
            for i in range(group):
                for f in range(4):
                    j = c * group + i
                    grad_v[f, :, j * 128 : (j + 1) * 128] = part[i * 32 + f * 8 : i * 32 + f * 8 + 8].astype(BF16)
            at = pl.ds(c * group * 128, group * 128)
            out = pltpu.make_async_copy(grad_v.at[:, :, at], grad_h.at[0, :, :, at], out_sem.at[c])
            out.start()
            outs.append(out)

    with jax.named_scope("member_sum_stage_2"):
        for copy in rs1:
            copy.wait_recv()

        for h, got, q, qf, me in ((h0, r0, q0, q0f, z_me), (h1, r1, q1, q1f, y_me)):

            def add_up(j, _, h=h, got=got, q=q, qf=qf, me=me):
                total = h[me * side + j].astype(F32)
                for d in range(side - 1):
                    total = total + got[d, j].astype(F32)
                qf[j] = total
                q[j] = total.astype(BF16)
                return 0

            lax.fori_loop(0, side, add_up, 0, unroll=2)
        rs2 = []
        for d in steps:
            z, y = along_z(d), along_y(d)
            rs2.append(remote(q0.at[y], t0.at[d - 1], rs2_s.at[0, d - 1], rs2_r.at[0, d - 1], at_y(y)))
            rs2.append(remote(q1.at[z], t1.at[d - 1], rs2_s.at[1, d - 1], rs2_r.at[1, d - 1], at_z(z)))
        for copy in rs2:
            copy.start()
        for copy in rs2:
            copy.wait_recv()
        total0, total1 = q0f[y_me], q1f[z_me]
        for d in range(side - 1):
            total0 = total0 + t0[d].astype(F32)
            total1 = total1 + t1[d].astype(F32)
        total = jnp.concatenate([total0, total1], axis=0) * (1.0 / math.sqrt(members))
        total = pltpu.roll(total, (128 - my_off) & 127, 1)
        total = jnp.where(lane32 < my_size, total, 0.0)
        for f, value in enumerate(fields_of(total)):
            inc_v[f] = value.astype(BF16)
        out = pltpu.make_async_copy(inc_v, inc_h, out_sem.at[n_groups])
        out.start()
        outs.append(out)

    with jax.named_scope("drain"):
        for copy in ag1 + ag2 + rs1 + rs2 + halo1 + halo2:
            copy.wait_send()
        for out in outs:
            out.wait()


def body(n_wide, n_lev, alpha, ens, htile, vloc, pattern, region_sizes, owner, cotangent):
    side = math.isqrt(n_wide)
    columns = alpha.shape[3]
    blocks = columns // 128
    slots = htile.shape[0]
    width = vloc.shape[1]
    group = min(8, blocks)
    n_groups = blocks // group
    dma = pltpu.SemaphoreType.DMA
    vmem = pltpu.VMEM
    ring = side - 1
    scratch = [
        vmem(alpha.shape, BF16), vmem(ens.shape, BF16), vmem(htile.shape, BF16), vmem(vloc.shape[::-1], F32),
        vmem(pattern.shape[::-1], I32), vmem((1, n_wide), I32), vmem((1, n_wide), I32), vmem(cotangent.shape, BF16),
        vmem((32, 128), I32), pltpu.SMEM((32, 128), I32),
        vmem((blocks, 32, 128), BF16),
        vmem((blocks * 32, slots * 128), BF16),
        vmem((128, slots * 128), BF16),
        vmem(vloc.shape, F32),
        vmem((blocks, 32, 128), F32),
        vmem((64, columns), BF16), vmem((64, columns), BF16),
        vmem((blocks, 32, 128), F32),
        vmem((n_wide, 16, 128), BF16), vmem((n_wide, 16, 128), BF16),
        vmem((ring, side, 16, 128), BF16), vmem((ring, side, 16, 128), BF16),
        vmem((side, 16, 128), BF16), vmem((side, 16, 128), BF16),
        vmem((side, 16, 128), F32), vmem((side, 16, 128), F32),
        vmem((ring, 16, 128), BF16), vmem((ring, 16, 128), BF16),
        vmem((n_wide, 16, 128), BF16), vmem((n_wide, 16, 128), BF16),
        vmem((n_wide, 32, 128), F32),
        vmem((blocks, 32, 128), F32),
        vmem((slots, blocks + 1, 32, 128), F32),
        vmem(alpha.shape[1:], BF16), vmem(cotangent.shape, BF16),
        dma((9,)), dma((n_groups + 1,)),
        *[dma((2, ring))] * 8,
        *[dma((n_groups,))] * 8,
    ]
    any_spec = pl.BlockSpec(memory_space=pl.ANY)
    return pl.pallas_call(
        functools.partial(kernel, side, n_lev, blocks, slots, n_wide, width),
        out_shape=(
            jax.ShapeDtypeStruct(cotangent.shape, BF16),
            jax.ShapeDtypeStruct(alpha.shape, BF16),
        ),
        in_specs=[any_spec] * 8,
        out_specs=(any_spec, any_spec),
        scratch_shapes=scratch,
        compiler_params=pltpu.CompilerParams(
            collective_id=0, has_side_effects=True, vmem_limit_bytes=VMEM_LIMIT
        ),
    )(
        alpha, ens, htile, vloc.T, pattern.T,
        region_sizes.reshape(1, n_wide), owner.reshape(1, n_wide), cotangent,
    )


def solution(mesh):
    placed = (
        P("wide", None, "lev", None),
        P("wide", None, "lev", None),
        P(),
        P(),
        P(),
        P(),
        P(),
        P(None, "lev", "wide"),
    )
    return jax.shard_map(
        functools.partial(body, mesh.shape["wide"], mesh.shape["lev"]),
        mesh=mesh,
        in_specs=placed,
        out_specs=(P(None, "lev", "wide"), P("wide", None, "lev", None)),
        check_vma=False,
    )
```

```python
import functools
import math

import jax
import jax.numpy as jnp
from jax import lax
from jax.experimental import pallas as pl
from jax.experimental.pallas import tpu as pltpu
from jax.sharding import PartitionSpec as P

REACH = 4
MESH = pl.DeviceIdType.MESH
F32 = jnp.float32
BF16 = jnp.bfloat16
I32 = jnp.int32
GATHER_AFTER = 1
VMEM_LIMIT = 60 * 1024 * 1024


def iota(shape, dim):
    return lax.broadcasted_iota(I32, shape, dim)


def halves_of(fields):
    first = iota(fields[0].shape, 0) < 4
    low, high = [], []
    for a, b in (fields[0:2], fields[2:4]):
        low.append(jnp.where(first, a, pltpu.roll(b, 4, 0)))
        high.append(jnp.where(first, pltpu.roll(a, 4, 0), b))
    return jnp.concatenate(low + high, axis=0)


def kernel(
    side, n_lev, blocks, slots, members, width,
    alpha_h, ens_h, htile_h, vloc_h, pattern_h, sizes_h, owner_h, cot_h,
    inc_h, grad_h,
    alpha_v, ens_v, tile_v, vloc_v, pat_v, size_v, own_v, tab_v, tab_s,
    a3, x, tiles_nt, band_v, e1, e2, p3, h0, h1, r0, r1, q0, q1, q0f, q1f, t0, t1,
    g0, g1, snap, mixed, run, grad_v, inc_v,
    local_sem, out_sem, ag1_s, ag1_r, ag2_s, ag2_r, rs1_s, rs1_r, rs2_s, rs2_r, up_s, up_r, dn_s, dn_r,
    bup_s, bup_r, bdn_s, bdn_r,
):
    n_wide = side * side
    w_me, l_me = lax.axis_index("wide"), lax.axis_index("lev")
    z_me, y_me = w_me // side, w_me % side
    upper, lower = lax.rem(l_me + 1, n_lev), lax.rem(l_me + n_lev - 1, n_lev)
    steps = sorted(range(1, side), key=lambda d: -min(d, side - d))

    def along_y(d):
        return lax.rem(y_me + d, side)

    def along_z(d):
        return lax.rem(z_me + d, side)

    def at_y(y):
        return (z_me * side + y, l_me)

    def at_z(z):
        return (z * side + y_me, l_me)

    def remote(src, dst, s, r, device):
        return pltpu.make_async_remote_copy(
            src_ref=src, dst_ref=dst, send_sem=s, recv_sem=r, device_id=device, device_id_type=MESH
        )

    with jax.named_scope("load_and_greet"):
        loads = [
            pltpu.make_async_copy(src, dst, local_sem.at[i])
            for i, (src, dst) in enumerate(
                (
                    (sizes_h, size_v), (owner_h, own_v), (pattern_h, pat_v),
                    (alpha_h, alpha_v), (htile_h, tile_v), (vloc_h, vloc_v), (ens_h, ens_v),
                )
            )
        ]
        for load in loads:
            load.start()
        barrier = pltpu.get_barrier_semaphore()
        friends = [at_y(along_y(d)) for d in steps] + [at_z(along_z(d)) for d in steps]
        friends += [(w_me, upper), (w_me, lower)]
        for friend in friends:
            pl.semaphore_signal(barrier, inc=1, device_id=friend, device_id_type=MESH)

    with jax.named_scope("cotangent_stage_1"):
        own0 = pltpu.make_async_copy(cot_h.at[0:2], g0.at[w_me], local_sem.at[8])
        own1 = pltpu.make_async_copy(cot_h.at[2:4], g1.at[y_me * side + z_me], local_sem.at[9])
        own0.start()
        own1.start()
        pl.semaphore_wait(barrier, len(friends))
        ag1 = []
        for d in steps:
            ag1.append(
                remote(cot_h.at[0:2], g0.at[w_me], ag1_s.at[0, d - 1], ag1_r.at[0, d - 1], at_y(along_y(d)))
            )
            ag1.append(
                remote(
                    cot_h.at[2:4], g1.at[y_me * side + z_me], ag1_s.at[1, d - 1], ag1_r.at[1, d - 1], at_z(along_z(d))
                )
            )
        for copy in ag1:
            copy.start()

    with jax.named_scope("tables"):
        for load in loads[:3]:
            load.wait()
        square = (n_wide, n_wide)
        rows, cols = iota(square, 0), iota(square, 1)
        size_b = jnp.broadcast_to(size_v[...], square)
        own_b = jnp.broadcast_to(own_v[...], square)
        start_c = jnp.sum(jnp.where(cols < rows, size_b, 0), axis=1, keepdims=True)
        size_c = jnp.sum(jnp.where(cols == rows, size_b, 0), axis=1, keepdims=True)
        own_c = jnp.sum(jnp.where(cols == rows, own_b, 0), axis=1, keepdims=True)
        held = own_c == cols
        base = 3 * slots
        tab_v[base : base + 1, 0:n_wide] = jnp.sum(jnp.where(held, start_c, 0), axis=0, keepdims=True)
        tab_v[base + 1 : base + 2, 0:n_wide] = jnp.sum(jnp.where(held, size_c, 0), axis=0, keepdims=True)
        tab_v[base + 2 : base + 3, 0:n_wide] = jnp.sum(jnp.where(cols == rows, start_c, 0), axis=0, keepdims=True)
        tab_v[base + 3 : base + 4, 0:n_wide] = size_v[...]
        tab_v[base + 4 : base + 5, 0:n_wide] = own_v[...]
        ends = iota((n_wide, blocks), 1) * 128 + 127
        covered = jnp.sum(jnp.where(start_c + size_c <= ends, 1, 0), axis=0, keepdims=True)
        tab_v[base + 5 : base + 6, 0:blocks] = jnp.minimum(covered, n_wide - 1)
        here, there = iota((blocks, blocks), 0), iota((blocks, blocks), 1)
        for k in range(slots):
            row = pat_v[k : k + 1, :]
            col = jnp.sum(jnp.where(here == there, row, 0), axis=1, keepdims=True)
            tab_v[k : k + 1, 0:blocks] = row
            before = jnp.max(jnp.where((col == row) & (here < there), here, -1), axis=0, keepdims=True)
            tab_v[slots + k : slots + k + 1, 0:blocks] = jnp.where(before < 0, blocks, before)
            last = jnp.max(jnp.where(col == there, here, -1), axis=0, keepdims=True)
            tab_v[2 * slots + k : 2 * slots + k + 1, 0:blocks] = jnp.where(last < 0, blocks, last)
        to_s = pltpu.make_async_copy(tab_v, tab_s, local_sem.at[7])
        to_s.start()
        to_s.wait()
        my_start = tab_s[base, w_me]
        my_size = tab_s[base + 1, w_me]
        my_off = my_start & 127

    lane32 = iota((32, 128), 1)

    def block_lanes(b):
        return pl.ds(pl.multiple_of(b * 128, 128), 128)

    with jax.named_scope("spread"):
        loads[3].wait()

        def split_alpha(b, _):
            a = alpha_v[0, :, :, block_lanes(b)].astype(F32)
            a3[b] = halves_of([a[f] for f in range(4)]).astype(BF16)
            return 0

        lax.fori_loop(0, blocks, split_alpha, 0, unroll=4)
        loads[4].wait()
        stacked = tile_v[...].reshape(slots * 128, 128)
        group = min(8, blocks)
        n_groups = blocks // group
        halo1 = []
        ag2 = []
        for c in range(n_groups):

            def pick(i, _, c=c):
                b = c * group + i
                at = pl.ds(pl.multiple_of(b * 32, 32), 32)
                for k in range(slots):
                    x[at, k * 128 : (k + 1) * 128] = a3[tab_s[k, b]]
                return 0

            lax.fori_loop(0, group, pick, 0, unroll=2)
            part = jnp.dot(
                x[c * group * 32 : (c + 1) * group * 32, :], stacked, preferred_element_type=F32
            ).astype(BF16)
            for i in range(group):
                b = c * group + i
                e1[0:32, b * 128 : (b + 1) * 128] = part[i * 32 : (i + 1) * 32]
            at = pl.ds(c * group * 128, group * 128)
            sends = [
                remote(e1.at[0:16, at], e1.at[48:64, at], dn_s.at[c], dn_r.at[c], (w_me, lower)),
                remote(e1.at[16:32, at], e1.at[32:48, at], up_s.at[c], up_r.at[c], (w_me, upper)),
            ]
            for copy in sends:
                copy.start()
            halo1 += sends
            if c == min(GATHER_AFTER, n_groups - 1):
                with jax.named_scope("cotangent_stage_2"):
                    for copy in ag1:
                        copy.wait_recv()
                    own0.wait()
                    own1.wait()
                    at0 = pl.ds(pl.multiple_of(z_me * side, side), side)
                    at1 = pl.ds(pl.multiple_of(y_me * side, side), side)
                    for d in steps:
                        ag2.append(
                            remote(g0.at[at0], g0.at[at0], ag2_s.at[0, d - 1], ag2_r.at[0, d - 1], at_z(along_z(d)))
                        )
                        ag2.append(
                            remote(g1.at[at1], g1.at[at1], ag2_s.at[1, d - 1], ag2_r.at[1, d - 1], at_y(along_y(d)))
                        )
                    for copy in ag2:
                        copy.start()

    with jax.named_scope("bands"):
        loads[5].wait()
        first_level = l_me * 8
        top = n_lev * 8
        half = iota((8, width), 0) < 4

        def pairs_of(v):
            r = pltpu.roll(v, 4, 0)
            return jnp.where(half, v, r), jnp.where(half, r, v)

        band_v[...] = jnp.transpose(vloc_v[...])
        band = band_v[pl.ds(pl.multiple_of(first_level, 8), 8), :]
        lows, highs = pairs_of(band)
        _, before = pairs_of(band_v[pl.ds(pl.multiple_of(jnp.maximum(first_level - 8, 0), 8), 8), :])
        after, _ = pairs_of(band_v[pl.ds(pl.multiple_of(jnp.minimum(first_level + 8, top - 8), 8), 8), :])

        def source_level(k):
            g, q = k // 16, k % 4
            return jnp.where(g == 0, q, jnp.where(g == 1, q + 4, jnp.where(g == 2, q - 4, q + 8)))

        def banded(values, inside, offset):
            total = jnp.zeros(offset.shape, F32)
            for o in range(width):
                column = jnp.broadcast_to(values[:, o : o + 1], offset.shape)
                total = total + jnp.where(inside & (offset == o), column, 0.0)
            return total

        def in_two(w):
            top_part = w.astype(BF16)
            rest = (w - top_part.astype(F32)).astype(BF16)
            return jnp.concatenate([top_part, rest], axis=0)

        shape = (32, 64)
        r, k = iota(shape, 0), iota(shape, 1)
        level_out, level_in = r % 8, source_level(k)
        inside = (r // 8 == (k % 16) // 4) & (first_level + level_in >= 0) & (first_level + level_in < top)
        down = in_two(banded(jnp.concatenate([band] * 4, axis=0), inside, level_in - level_out + REACH))
        shape = (128, 128)
        k, r = iota(shape, 0), iota(shape, 1)
        level_out, level_in = r % 8, source_level(k)
        inside = (r // 8 == (k % 16) // 4) & (first_level + level_in >= 0) & (first_level + level_in < top)
        inside = inside & (k < 64) & (r < 32)
        rows_in = [lows, lows, highs, highs, before, before, after, after] + [jnp.zeros((8, width), F32)] * 8
        up = banded(jnp.concatenate(rows_in, axis=0), inside, level_out - level_in + REACH)
        up = in_two(jnp.transpose(up)[0:32, 0:64])

    with jax.named_scope("ensemble"):
        loads[6].wait()

        def ens_block(b):
            return ens_v[0, :, :, block_lanes(b)].astype(F32).reshape(32, 128)

        for k in range(slots):
            tiles_nt[:, k * 128 : (k + 1) * 128] = tile_v[k]

    with jax.named_scope("mix_down"):
        wide_mix = min(4, blocks)
        mixes = group // wide_mix

        def down_step(i, _):
            at = pl.ds(pl.multiple_of(i * wide_mix * 128, wide_mix * 128), wide_mix * 128)
            both = jnp.dot(down, e1[:, at], preferred_element_type=F32)
            local = (both[:32] + both[32:]).astype(BF16).astype(F32)
            for j in range(wide_mix):
                b = i * wide_mix + j
                p3[b] = local[:, j * 128 : (j + 1) * 128] * ens_block(b)
            return 0

        for c in range(n_groups):
            for copy in halo1[2 * c : 2 * c + 2]:
                copy.wait_recv()
            lax.fori_loop(c * mixes, (c + 1) * mixes, down_step, 0, unroll=mixes)

    with jax.named_scope("member_sum_stage_1"):

        def share(w, _):
            start = tab_s[base, w]
            blk = lax.shift_right_logical(start, 7)
            t = jnp.where(lane32 >= (start & 127), p3[blk], p3[jnp.minimum(blk + 1, blocks - 1)]).astype(BF16)
            h0[w] = t[:16]
            h1[lax.rem(w, side) * side + lax.div(w, side)] = t[16:]
            return 0

        lax.fori_loop(0, n_wide, share, 0, unroll=4)
        rs1 = []
        for d in steps:
            z, y = along_z(d), along_y(d)
            at0 = pl.ds(pl.multiple_of(z * side, side), side)
            at1 = pl.ds(pl.multiple_of(y * side, side), side)
            rs1.append(remote(h0.at[at0], r0.at[d - 1], rs1_s.at[0, d - 1], rs1_r.at[0, d - 1], at_z(z)))
            rs1.append(remote(h1.at[at1], r1.at[d - 1], rs1_s.at[1, d - 1], rs1_r.at[1, d - 1], at_y(y)))
        for copy in rs1:
            copy.start()

    with jax.named_scope("scaled"):
        for copy in ag2:
            copy.wait_recv()

        def paint(r, acc):
            o = tab_s[base + 4, r]
            start, size = tab_s[base + 2, r] & 127, tab_s[base + 3, r]
            first = g0[o].astype(F32).reshape(16, 128)
            second = g1[(o & (side - 1)) * side + lax.div(o, side)].astype(F32).reshape(16, 128)
            tile = pltpu.roll(jnp.concatenate([first, second], axis=0), start, 1)
            acc = jnp.where((lane32 >= start) & (lane32 < start + size), tile, acc)
            snap[r] = acc
            return jnp.where(lane32 < start + size - 128, tile, acc)

        lax.fori_loop(0, n_wide, paint, jnp.zeros((32, 128), F32), unroll=4)
        halo2 = []
        for c in range(n_groups):

            def scale(i, _, c=c):
                b = c * group + i
                s = ens_block(b) * snap[tab_s[base + 5, b]]
                e2[0:32, block_lanes(b)] = halves_of([s[8 * f : 8 * f + 8] for f in range(4)]).astype(BF16)
                return 0

            lax.fori_loop(0, group, scale, 0, unroll=4)
            at = pl.ds(c * group * 128, group * 128)
            sends = [
                remote(e2.at[0:16, at], e2.at[48:64, at], bdn_s.at[c], bdn_r.at[c], (w_me, lower)),
                remote(e2.at[16:32, at], e2.at[32:48, at], bup_s.at[c], bup_r.at[c], (w_me, upper)),
            ]
            for copy in sends:
                copy.start()
            halo2 += sends

    with jax.named_scope("mix_up"):
        for k in range(slots):
            run[k, blocks] = jnp.zeros((32, 128), F32)
        def up_step(i, _):
            at = pl.ds(pl.multiple_of(i * wide_mix * 128, wide_mix * 128), wide_mix * 128)
            both = jnp.dot(up, e2[:, at], preferred_element_type=F32)
            local = (both[:32] + both[32:]).astype(BF16).astype(F32)
            for j in range(wide_mix):
                mixed[i * wide_mix + j] = local[:, j * 128 : (j + 1) * 128]
            return 0

        for c in range(n_groups):
            for copy in halo2[2 * c : 2 * c + 2]:
                copy.wait_recv()
            lax.fori_loop(c * mixes, (c + 1) * mixes, up_step, 0, unroll=mixes)

        def link(b, _):
            m = mixed[b]
            earlier = [run[k, tab_s[slots + k, b]] for k in range(slots)]
            for k in range(slots):
                run[k, b] = m + earlier[k]
            return 0

        lax.fori_loop(0, blocks, link, 0)

    with jax.named_scope("member_sum_stage_2"):
        for copy in rs1:
            copy.wait_recv()

        for h, got, q, qf, me in ((h0, r0, q0, q0f, z_me), (h1, r1, q1, q1f, y_me)):

            def add_up(j, _, h=h, got=got, q=q, qf=qf, me=me):
                total = h[me * side + j].astype(F32)
                for d in range(side - 1):
                    total = total + got[d, j].astype(F32)
                qf[j] = total
                q[j] = total.astype(BF16)
                return 0

            lax.fori_loop(0, side, add_up, 0, unroll=2)
        rs2 = []
        for d in steps:
            z, y = along_z(d), along_y(d)
            rs2.append(remote(q0.at[y], t0.at[d - 1], rs2_s.at[0, d - 1], rs2_r.at[0, d - 1], at_y(y)))
            rs2.append(remote(q1.at[z], t1.at[d - 1], rs2_s.at[1, d - 1], rs2_r.at[1, d - 1], at_z(z)))
        for copy in rs2:
            copy.start()

    with jax.named_scope("gradient"):
        outs = []
        for c in range(n_groups):

            def pick_back(i, _, c=c):
                j = c * group + i
                at = pl.ds(pl.multiple_of(j * 32, 32), 32)
                for k in range(slots):
                    x[at, k * 128 : (k + 1) * 128] = run[k, tab_s[2 * slots + k, j]].astype(BF16)
                return 0

            lax.fori_loop(0, group, pick_back, 0, unroll=2)
            part = lax.dot_general(
                x[c * group * 32 : (c + 1) * group * 32, :],
                tiles_nt[...],
                (((1,), (1,)), ((), ())),
                preferred_element_type=F32,
            )
            for i in range(group):
                for f in range(4):
                    j = c * group + i
                    grad_v[f, :, j * 128 : (j + 1) * 128] = part[i * 32 + f * 8 : i * 32 + f * 8 + 8].astype(BF16)
            at = pl.ds(c * group * 128, group * 128)
            out = pltpu.make_async_copy(grad_v.at[:, :, at], grad_h.at[0, :, :, at], out_sem.at[c])
            out.start()
            outs.append(out)

    with jax.named_scope("increment"):
        for copy in rs2:
            copy.wait_recv()
        total0, total1 = q0f[y_me], q1f[z_me]
        for d in range(side - 1):
            total0 = total0 + t0[d].astype(F32)
            total1 = total1 + t1[d].astype(F32)
        total = jnp.concatenate([total0, total1], axis=0) * (1.0 / math.sqrt(members))
        total = pltpu.roll(total, (128 - my_off) & 127, 1)
        total = jnp.where(lane32 < my_size, total, 0.0)
        for f in range(4):
            inc_v[f] = total[8 * f : 8 * f + 8].astype(BF16)
        out = pltpu.make_async_copy(inc_v, inc_h, out_sem.at[n_groups])
        out.start()
        outs.append(out)

    with jax.named_scope("drain"):
        for copy in ag1 + ag2 + rs1 + rs2 + halo1 + halo2:
            copy.wait_send()
        for out in outs:
            out.wait()


def hand_over(inc_h, grad_h, inc_out, grad_out, sem):
    copies = [pltpu.make_async_copy(inc_h, inc_out, sem.at[0])]
    copies += [pltpu.make_async_copy(grad_h.at[0, f], grad_out.at[0, f], sem.at[1 + f]) for f in range(4)]
    for copy in copies:
        copy.start()
    for copy in copies:
        copy.wait()


def body(n_wide, n_lev, alpha, ens, htile, vloc, pattern, region_sizes, owner, cotangent):
    side = math.isqrt(n_wide)
    columns = alpha.shape[3]
    blocks = columns // 128
    slots = htile.shape[0]
    width = vloc.shape[1]
    group = min(8, blocks)
    n_groups = blocks // group
    dma = pltpu.SemaphoreType.DMA
    vmem = pltpu.VMEM
    ring = side - 1
    scratch = [
        vmem(alpha.shape, BF16), vmem(ens.shape, BF16), vmem(htile.shape, BF16), vmem(vloc.shape[::-1], F32),
        vmem(pattern.shape[::-1], I32), vmem((1, n_wide), I32), vmem((1, n_wide), I32),
        vmem((32, 128), I32), pltpu.SMEM((32, 128), I32),
        vmem((blocks, 32, 128), BF16),
        vmem((blocks * 32, slots * 128), BF16),
        vmem((128, slots * 128), BF16),
        vmem(vloc.shape, F32),
        vmem((64, columns), BF16), vmem((64, columns), BF16),
        vmem((blocks, 32, 128), F32),
        vmem((n_wide, 16, 128), BF16), vmem((n_wide, 16, 128), BF16),
        vmem((ring, side, 16, 128), BF16), vmem((ring, side, 16, 128), BF16),
        vmem((side, 16, 128), BF16), vmem((side, 16, 128), BF16),
        vmem((side, 16, 128), F32), vmem((side, 16, 128), F32),
        vmem((ring, 16, 128), BF16), vmem((ring, 16, 128), BF16),
        vmem((n_wide, 2, 8, 128), BF16), vmem((n_wide, 2, 8, 128), BF16),
        vmem((n_wide, 32, 128), F32),
        vmem((blocks, 32, 128), F32),
        vmem((slots, blocks + 1, 32, 128), F32),
        vmem(alpha.shape[1:], BF16), vmem(cotangent.shape, BF16),
        dma((10,)), dma((n_groups + 1,)),
        *[dma((2, ring))] * 8,
        *[dma((n_groups,))] * 8,
    ]
    any_spec = pl.BlockSpec(memory_space=pl.ANY)
    shapes = (jax.ShapeDtypeStruct(cotangent.shape, BF16), jax.ShapeDtypeStruct(alpha.shape, BF16))
    results = pl.pallas_call(
        functools.partial(kernel, side, n_lev, blocks, slots, n_wide, width),
        out_shape=shapes,
        in_specs=[any_spec] * 8,
        out_specs=(any_spec, any_spec),
        scratch_shapes=scratch,
        compiler_params=pltpu.CompilerParams(
            collective_id=0, has_side_effects=True, vmem_limit_bytes=VMEM_LIMIT
        ),
    )(
        alpha, ens, htile, vloc.T, pattern.T,
        region_sizes.reshape(1, n_wide), owner.reshape(1, n_wide), cotangent,
    )
    return results


def solution(mesh):
    placed = (
        P("wide", None, "lev", None),
        P("wide", None, "lev", None),
        P(),
        P(),
        P(),
        P(),
        P(),
        P(None, "lev", "wide"),
    )
    return jax.shard_map(
        functools.partial(body, mesh.shape["wide"], mesh.shape["lev"]),
        mesh=mesh,
        in_specs=placed,
        out_specs=(P(None, "lev", "wide"), P("wide", None, "lev", None)),
        check_vma=False,
    )
```

```python
import functools
import math

import jax
import jax.numpy as jnp
from jax import lax
from jax.experimental import pallas as pl
from jax.experimental.pallas import tpu as pltpu
from jax.sharding import PartitionSpec as P

REACH = 4
MESH = pl.DeviceIdType.MESH
F32 = jnp.float32
BF16 = jnp.bfloat16
I32 = jnp.int32
GATHER_AFTER = 1
VMEM_LIMIT = 60 * 1024 * 1024


def iota(shape, dim):
    return lax.broadcasted_iota(I32, shape, dim)


def halves_of(fields):
    first = iota(fields[0].shape, 0) < 4
    low, high = [], []
    for a, b in (fields[0:2], fields[2:4]):
        low.append(jnp.where(first, a, pltpu.roll(b, 4, 0)))
        high.append(jnp.where(first, pltpu.roll(a, 4, 0), b))
    return jnp.concatenate(low + high, axis=0)


def kernel(
    side, n_lev, blocks, slots, members, width,
    alpha_h, ens_h, htile_h, vloc_h, pattern_h, sizes_h, owner_h, cot_h,
    inc_h, grad_h,
    alpha_v, ens_v, tile_v, vloc_v, pat_v, size_v, own_v, tab_v, tab_s,
    a3, x, tiles_nt, band_v, e1, e2, p3, h0, h1, r0, r1, q0, q1, q0f, q1f, t0, t1,
    g0, g1, snap, run, grad_v, inc_v,
    local_sem, out_sem, ag1_s, ag1_r, ag2_s, ag2_r, rs1_s, rs1_r, rs2_s, rs2_r, up_s, up_r, dn_s, dn_r,
    bup_s, bup_r, bdn_s, bdn_r,
):
    n_wide = side * side
    bits = side.bit_length() - 1
    w_me, l_me = lax.axis_index("wide"), lax.axis_index("lev")
    z_me, y_me = w_me // side, w_me % side
    upper, lower = lax.rem(l_me + 1, n_lev), lax.rem(l_me + n_lev - 1, n_lev)
    steps = sorted(range(1, side), key=lambda d: -min(d, side - d))
    order = sorted(range(side), key=lambda d: (min(d, side - d), d))
    place = {d: p for p, d in enumerate(order)}
    cuts = (0, 1, min(5, side), side)
    groups = [(g, a, b) for g, (a, b) in enumerate(zip(cuts, cuts[1:])) if a < b]

    def along_y(d):
        return lax.rem(y_me + d, side)

    def along_z(d):
        return lax.rem(z_me + d, side)

    def at_y(y):
        return (z_me * side + y, l_me)

    def at_z(z):
        return (z * side + y_me, l_me)

    def remote(src, dst, s, r, device):
        return pltpu.make_async_remote_copy(
            src_ref=src, dst_ref=dst, send_sem=s, recv_sem=r, device_id=device, device_id_type=MESH
        )

    with jax.named_scope("load_and_greet"):
        loads = [
            pltpu.make_async_copy(src, dst, local_sem.at[i])
            for i, (src, dst) in enumerate(
                (
                    (sizes_h, size_v), (owner_h, own_v), (pattern_h, pat_v),
                    (alpha_h, alpha_v), (htile_h, tile_v), (vloc_h, vloc_v), (ens_h, ens_v),
                )
            )
        ]
        for load in loads:
            load.start()
        barrier = pltpu.get_barrier_semaphore()
        friends = [at_y(along_y(d)) for d in steps] + [at_z(along_z(d)) for d in steps]
        friends += [(w_me, upper), (w_me, lower)]
        for friend in friends:
            pl.semaphore_signal(barrier, inc=1, device_id=friend, device_id_type=MESH)

    with jax.named_scope("cotangent_stage_1"):
        own0 = pltpu.make_async_copy(cot_h.at[0:2], g0.at[z_me * side], local_sem.at[8])
        own1 = pltpu.make_async_copy(cot_h.at[2:4], g1.at[y_me * side], local_sem.at[9])
        own0.start()
        own1.start()
        pl.semaphore_wait(barrier, len(friends))
        ag1, ag2 = {}, []
        for d in steps:
            p = place[side - d]
            to0, to1 = g0.at[z_me * side + p], g1.at[y_me * side + p]
            ag1[p] = (
                remote(cot_h.at[0:2], to0, ag1_s.at[0, d - 1], ag1_r.at[0, d - 1], at_y(along_y(d))),
                remote(cot_h.at[2:4], to1, ag1_s.at[1, d - 1], ag1_r.at[1, d - 1], at_z(along_z(d))),
            )
            for copy in ag1[p]:
                copy.start()

        def forward(g, a, b):
            for p in range(max(a, 1), b):
                for copy in ag1[p]:
                    copy.wait_recv()
            at0, at1 = pl.ds(z_me * side + a, b - a), pl.ds(y_me * side + a, b - a)
            for d in steps:
                pair = (
                    remote(
                        cot_h.at[0:2] if g == 0 else g0.at[at0],
                        g0.at[z_me * side] if g == 0 else g0.at[at0],
                        ag2_s.at[0, g, d - 1], ag2_r.at[0, g, d - 1], at_z(along_z(d)),
                    ),
                    remote(
                        cot_h.at[2:4] if g == 0 else g1.at[at1],
                        g1.at[y_me * side] if g == 0 else g1.at[at1],
                        ag2_s.at[1, g, d - 1], ag2_r.at[1, g, d - 1], at_y(along_y(d)),
                    ),
                )
                for copy in pair:
                    copy.start()
                ag2.extend(pair)

        forward(*groups[0])

    with jax.named_scope("tables"):
        for load in loads[:3]:
            load.wait()
        square = (n_wide, n_wide)
        rows, cols = iota(square, 0), iota(square, 1)
        size_b = jnp.broadcast_to(size_v[...], square)
        own_b = jnp.broadcast_to(own_v[...], square)
        start_c = jnp.sum(jnp.where(cols < rows, size_b, 0), axis=1, keepdims=True)
        size_c = jnp.sum(jnp.where(cols == rows, size_b, 0), axis=1, keepdims=True)
        own_c = jnp.sum(jnp.where(cols == rows, own_b, 0), axis=1, keepdims=True)
        held = own_c == cols
        base = 3 * slots
        tab_v[base : base + 1, 0:n_wide] = jnp.sum(jnp.where(held, start_c, 0), axis=0, keepdims=True)
        tab_v[base + 1 : base + 2, 0:n_wide] = jnp.sum(jnp.where(held, size_c, 0), axis=0, keepdims=True)
        tab_v[base + 2 : base + 3, 0:n_wide] = jnp.sum(jnp.where(cols == rows, start_c, 0), axis=0, keepdims=True)
        tab_v[base + 3 : base + 4, 0:n_wide] = size_v[...]


        def near(d):
            return jnp.where(2 * d <= side, jnp.maximum(2 * d - 1, 0), 2 * (side - d))

        z_own, y_own = lax.shift_right_logical(own_v[...], bits), own_v[...] & (side - 1)
        tab_v[base + 4 : base + 5, 0:n_wide] = z_own * side + near((y_own - y_me) & (side - 1))
        tab_v[base + 6 : base + 7, 0:n_wide] = y_own * side + near((z_own - z_me) & (side - 1))
        ends = iota((n_wide, blocks), 1) * 128 + 127
        covered = jnp.sum(jnp.where(start_c + size_c <= ends, 1, 0), axis=0, keepdims=True)
        tab_v[base + 5 : base + 6, 0:blocks] = jnp.minimum(covered, n_wide - 1)
        here, there = iota((blocks, blocks), 0), iota((blocks, blocks), 1)
        for k in range(slots):
            row = pat_v[k : k + 1, :]
            col = jnp.sum(jnp.where(here == there, row, 0), axis=1, keepdims=True)
            tab_v[k : k + 1, 0:blocks] = row
            before = jnp.max(jnp.where((col == row) & (here < there), here, -1), axis=0, keepdims=True)
            tab_v[slots + k : slots + k + 1, 0:blocks] = jnp.where(before < 0, blocks, before)
            last = jnp.max(jnp.where(col == there, here, -1), axis=0, keepdims=True)
            tab_v[2 * slots + k : 2 * slots + k + 1, 0:blocks] = jnp.where(last < 0, blocks, last)
        to_s = pltpu.make_async_copy(tab_v, tab_s, local_sem.at[7])
        to_s.start()
        to_s.wait()
        my_start = tab_s[base, w_me]
        my_size = tab_s[base + 1, w_me]
        my_off = my_start & 127

    lane16, lane32 = iota((16, 128), 1), iota((32, 128), 1)

    def block_lanes(b):
        return pl.ds(pl.multiple_of(b * 128, 128), 128)

    with jax.named_scope("spread"):
        loads[3].wait()

        def split_alpha(b, _):
            a = alpha_v[0, :, :, block_lanes(b)].astype(F32)
            a3[b] = halves_of([a[f] for f in range(4)]).astype(BF16)
            return 0

        lax.fori_loop(0, blocks, split_alpha, 0, unroll=8)
        loads[4].wait()
        stacked = tile_v[...].reshape(slots * 128, 128)
        group = min(8, blocks)
        n_groups = blocks // group
        halo1 = []
        for c in range(n_groups):

            def pick(i, _, c=c):
                b = c * group + i
                at = pl.ds(pl.multiple_of(b * 32, 32), 32)
                for k in range(slots):
                    x[at, k * 128 : (k + 1) * 128] = a3[tab_s[k, b]]
                return 0

            lax.fori_loop(0, group, pick, 0, unroll=8)
            part = jnp.dot(
                x[c * group * 32 : (c + 1) * group * 32, :], stacked, preferred_element_type=F32
            ).astype(BF16)
            for i in range(group):
                b = c * group + i
                e1[0:32, b * 128 : (b + 1) * 128] = part[i * 32 : (i + 1) * 32]
            at = pl.ds(c * group * 128, group * 128)
            sends = [
                remote(e1.at[0:16, at], e1.at[48:64, at], dn_s.at[c], dn_r.at[c], (w_me, lower)),
                remote(e1.at[16:32, at], e1.at[32:48, at], up_s.at[c], up_r.at[c], (w_me, upper)),
            ]
            for copy in sends:
                copy.start()
            halo1 += sends
            if c == min(GATHER_AFTER, n_groups - 1):
                for group_of in groups[1:2]:
                    forward(*group_of)

    with jax.named_scope("bands"):
        loads[5].wait()
        first_level = l_me * 8
        top = n_lev * 8
        half = iota((8, width), 0) < 4

        def pairs_of(v):
            r = pltpu.roll(v, 4, 0)
            return jnp.where(half, v, r), jnp.where(half, r, v)

        band_v[...] = jnp.transpose(vloc_v[...])
        band = band_v[pl.ds(pl.multiple_of(first_level, 8), 8), :]
        lows, highs = pairs_of(band)
        _, before = pairs_of(band_v[pl.ds(pl.multiple_of(jnp.maximum(first_level - 8, 0), 8), 8), :])
        after, _ = pairs_of(band_v[pl.ds(pl.multiple_of(jnp.minimum(first_level + 8, top - 8), 8), 8), :])

        def source_level(k):
            g, q = k // 16, k % 4
            return jnp.where(g == 0, q, jnp.where(g == 1, q + 4, jnp.where(g == 2, q - 4, q + 8)))

        def banded(values, inside, offset):
            total = jnp.zeros(offset.shape, F32)
            for o in range(width):
                column = jnp.broadcast_to(values[:, o : o + 1], offset.shape)
                total = total + jnp.where(inside & (offset == o), column, 0.0)
            return total

        def in_two(w):
            top_part = w.astype(BF16)
            rest = (w - top_part.astype(F32)).astype(BF16)
            return jnp.concatenate([top_part, rest], axis=0)

        shape = (32, 64)
        r, k = iota(shape, 0), iota(shape, 1)
        level_out, level_in = r % 8, source_level(k)
        inside = (r // 8 == (k % 16) // 4) & (first_level + level_in >= 0) & (first_level + level_in < top)
        down = in_two(banded(jnp.concatenate([band] * 4, axis=0), inside, level_in - level_out + REACH))
        shape = (128, 128)
        k, r = iota(shape, 0), iota(shape, 1)
        level_out, level_in = r % 8, source_level(k)
        inside = (r // 8 == (k % 16) // 4) & (first_level + level_in >= 0) & (first_level + level_in < top)
        inside = inside & (k < 64) & (r < 32)
        rows_in = [lows, lows, highs, highs, before, before, after, after] + [jnp.zeros((8, width), F32)] * 8
        up = banded(jnp.concatenate(rows_in, axis=0), inside, level_out - level_in + REACH)
        up = in_two(jnp.transpose(up)[0:32, 0:64])
        for group_of in groups[2:]:
            forward(*group_of)

    with jax.named_scope("ensemble"):
        loads[6].wait()

        def ens_block(b):
            return ens_v[0, :, :, block_lanes(b)].astype(F32).reshape(32, 128)

        for k in range(slots):
            tiles_nt[:, k * 128 : (k + 1) * 128] = tile_v[k]

    with jax.named_scope("mix_down"):
        wide_mix = min(4, blocks)
        mixes = group // wide_mix

        def down_step(i, _):
            at = pl.ds(pl.multiple_of(i * wide_mix * 128, wide_mix * 128), wide_mix * 128)
            both = jnp.dot(down, e1[:, at], preferred_element_type=F32)
            local = (both[:32] + both[32:]).astype(BF16).astype(F32)
            for j in range(wide_mix):
                b = i * wide_mix + j
                p3[b] = local[:, j * 128 : (j + 1) * 128] * ens_block(b)
            return 0

        for c in range(n_groups):
            for copy in halo1[2 * c : 2 * c + 2]:
                copy.wait_recv()
            lax.fori_loop(c * mixes, (c + 1) * mixes, down_step, 0, unroll=mixes)

    with jax.named_scope("member_sum_stage_1"):

        def share(w, rows):
            start = tab_s[base, w]
            blk = lax.shift_right_logical(start, 7)
            first, second = p3[blk, rows], p3[jnp.minimum(blk + 1, blocks - 1), rows]
            return jnp.where(lane16 >= (start & 127), first, second).astype(BF16)

        rs1 = {}
        for g, a, b in reversed(groups):

            def shares(i, _, a=a, b=b):
                for p in range(a, b):
                    h0[i * side + p] = share(i * side + along_y(order[p]), slice(0, 16))
                    h1[i * side + p] = share(along_z(order[p]) * side + i, slice(16, 32))
                return 0

            lax.fori_loop(0, side, shares, 0, unroll=2)
            rs1[g] = []
            for d in steps:
                z, y = along_z(d), along_y(d)
                at0, at1, to = pl.ds(z * side + a, b - a), pl.ds(y * side + a, b - a), pl.ds(a, b - a)
                rs1[g].append(
                    remote(h0.at[at0], r0.at[d - 1, to], rs1_s.at[0, g, d - 1], rs1_r.at[0, g, d - 1], at_z(z))
                )
                rs1[g].append(
                    remote(h1.at[at1], r1.at[d - 1, to], rs1_s.at[1, g, d - 1], rs1_r.at[1, g, d - 1], at_y(y))
                )
            for copy in rs1[g]:
                copy.start()

        rs2 = []

        def finish(g, a, b):
            for copy in rs1[g]:
                copy.wait_recv()
            for h, got, q, qf, me in ((h0, r0, q0, q0f, z_me), (h1, r1, q1, q1f, y_me)):
                for p in range(a, b):
                    total = h[me * side + p].astype(F32)
                    for d in range(side - 1):
                        total = total + got[d, p].astype(F32)
                    if p == 0:
                        qf[...] = total
                    else:
                        q[p] = total.astype(BF16)
            for p in reversed(range(max(a, 1), b)):
                d = order[p]
                pair = (
                    remote(q0.at[p], t0.at[d - 1], rs2_s.at[0, d - 1], rs2_r.at[0, d - 1], at_y(along_y(d))),
                    remote(q1.at[p], t1.at[d - 1], rs2_s.at[1, d - 1], rs2_r.at[1, d - 1], at_z(along_z(d))),
                )
                for copy in pair:
                    copy.start()
                rs2.extend(pair)

    with jax.named_scope("scaled"):
        own0.wait()
        own1.wait()
        for copy in ag2:
            copy.wait_recv()

        def paint(r, acc):
            start, size = tab_s[base + 2, r] & 127, tab_s[base + 3, r]
            first = g0[tab_s[base + 4, r]].astype(F32).reshape(16, 128)
            second = g1[tab_s[base + 6, r]].astype(F32).reshape(16, 128)
            tile = pltpu.roll(jnp.concatenate([first, second], axis=0), start, 1)
            acc = jnp.where((lane32 >= start) & (lane32 < start + size), tile, acc)
            snap[r] = acc
            return jnp.where(lane32 < start + size - 128, tile, acc)

        lax.fori_loop(0, n_wide, paint, jnp.zeros((32, 128), F32), unroll=8)
        for k in range(slots):
            run[k, blocks] = jnp.zeros((32, 128), F32)

        def link(b, _):
            s = ens_block(b) * snap[tab_s[base + 5, b]]
            s = halves_of([s[8 * f : 8 * f + 8] for f in range(4)]).astype(BF16).astype(F32)
            earlier = [run[k, tab_s[slots + k, b]] for k in range(slots)]
            for k in range(slots):
                run[k, b] = s + earlier[k]
            return 0

        lax.fori_loop(0, blocks, link, 0, unroll=4)

    with jax.named_scope("member_sum_far"):
        for group_of in groups[2:]:
            finish(*group_of)

    with jax.named_scope("tile_product"):
        halo2 = []
        for c in range(n_groups):

            def pick_back(i, _, c=c):
                j = c * group + i
                at = pl.ds(pl.multiple_of(j * 32, 32), 32)
                for k in range(slots):
                    x[at, k * 128 : (k + 1) * 128] = run[k, tab_s[2 * slots + k, j]].astype(BF16)
                return 0

            lax.fori_loop(0, group, pick_back, 0, unroll=8)
            part = lax.dot_general(
                x[c * group * 32 : (c + 1) * group * 32, :],
                tiles_nt[...],
                (((1,), (1,)), ((), ())),
                preferred_element_type=F32,
            ).astype(BF16)
            for i in range(group):
                j = c * group + i
                e2[0:32, j * 128 : (j + 1) * 128] = part[i * 32 : (i + 1) * 32]
            at = pl.ds(c * group * 128, group * 128)
            sends = [
                remote(e2.at[0:16, at], e2.at[48:64, at], bdn_s.at[c], bdn_r.at[c], (w_me, lower)),
                remote(e2.at[16:32, at], e2.at[32:48, at], bup_s.at[c], bup_r.at[c], (w_me, upper)),
            ]
            for copy in sends:
                copy.start()
            halo2 += sends

    with jax.named_scope("member_sum_stage_2"):
        for group_of in reversed(groups[:2]):
            finish(*group_of)

    with jax.named_scope("mix_up"):
        outs = []

        def up_step(i, _):
            at = pl.ds(pl.multiple_of(i * wide_mix * 128, wide_mix * 128), wide_mix * 128)
            both = jnp.dot(up, e2[:, at], preferred_element_type=F32)
            local = (both[:32] + both[32:]).astype(BF16)
            for f in range(4):
                grad_v[f, :, at] = local[8 * f : 8 * f + 8]
            return 0

        for c in range(n_groups):
            for copy in halo2[2 * c : 2 * c + 2]:
                copy.wait_recv()
            lax.fori_loop(c * mixes, (c + 1) * mixes, up_step, 0, unroll=mixes)
            at = pl.ds(c * group * 128, group * 128)
            out = pltpu.make_async_copy(grad_v.at[:, :, at], grad_h.at[0, :, :, at], out_sem.at[c])
            out.start()
            outs.append(out)

    with jax.named_scope("increment"):
        for copy in rs2:
            copy.wait_recv()
        total0, total1 = q0f[...], q1f[...]
        for d in range(side - 1):
            total0 = total0 + t0[d].astype(F32)
            total1 = total1 + t1[d].astype(F32)
        total = jnp.concatenate([total0, total1], axis=0) * (1.0 / math.sqrt(members))
        total = pltpu.roll(total, (128 - my_off) & 127, 1)
        total = jnp.where(lane32 < my_size, total, 0.0)
        for f in range(4):
            inc_v[f] = total[8 * f : 8 * f + 8].astype(BF16)
        out = pltpu.make_async_copy(inc_v, inc_h, out_sem.at[n_groups])
        out.start()
        outs.append(out)

    with jax.named_scope("drain"):
        sent = [copy for pair in ag1.values() for copy in pair] + [copy for part in rs1.values() for copy in part]
        for copy in sent + ag2 + rs2 + halo1 + halo2:
            copy.wait_send()
        for out in outs:
            out.wait()


def hand_over(inc_h, grad_h, inc_out, grad_out, sem):
    copies = [pltpu.make_async_copy(inc_h, inc_out, sem.at[0])]
    copies += [pltpu.make_async_copy(grad_h.at[0, f], grad_out.at[0, f], sem.at[1 + f]) for f in range(4)]
    for copy in copies:
        copy.start()
    for copy in copies:
        copy.wait()


def hand_over(inc_h, grad_h, inc_out, grad_out, sem):
    copies = [pltpu.make_async_copy(inc_h, inc_out, sem.at[0])]
    copies += [pltpu.make_async_copy(grad_h.at[0, f], grad_out.at[0, f], sem.at[1 + f]) for f in range(4)]
    for copy in copies:
        copy.start()
    for copy in copies:
        copy.wait()


def hand_over(inc_v, grad_v, inc_out, grad_out):
    inc_out[...] = inc_v[...]
    grad_out[...] = grad_v[...]


def body(n_wide, n_lev, alpha, ens, htile, vloc, pattern, region_sizes, owner, cotangent):
    side = math.isqrt(n_wide)
    columns = alpha.shape[3]
    blocks = columns // 128
    slots = htile.shape[0]
    width = vloc.shape[1]
    group = min(8, blocks)
    n_groups = blocks // group
    dma = pltpu.SemaphoreType.DMA
    vmem = pltpu.VMEM
    ring = side - 1
    scratch = [
        vmem(alpha.shape, BF16), vmem(ens.shape, BF16), vmem(htile.shape, BF16), vmem(vloc.shape[::-1], F32),
        vmem(pattern.shape[::-1], I32), vmem((1, n_wide), I32), vmem((1, n_wide), I32),
        vmem((32, 128), I32), pltpu.SMEM((32, 128), I32),
        vmem((blocks, 32, 128), BF16),
        vmem((blocks * 32, slots * 128), BF16),
        vmem((128, slots * 128), BF16),
        vmem(vloc.shape, F32),
        vmem((64, columns), BF16), vmem((64, columns), BF16),
        vmem((blocks, 32, 128), F32),
        vmem((n_wide, 16, 128), BF16), vmem((n_wide, 16, 128), BF16),
        vmem((ring, side, 16, 128), BF16), vmem((ring, side, 16, 128), BF16),
        vmem((side, 16, 128), BF16), vmem((side, 16, 128), BF16),
        vmem((16, 128), F32), vmem((16, 128), F32),
        vmem((ring, 16, 128), BF16), vmem((ring, 16, 128), BF16),
        vmem((n_wide, 2, 8, 128), BF16), vmem((n_wide, 2, 8, 128), BF16),
        vmem((n_wide, 32, 128), F32),
        vmem((slots, blocks + 1, 32, 128), F32),
        vmem(alpha.shape[1:], BF16), vmem(cotangent.shape, BF16),
        dma((10,)), dma((n_groups + 1,)),
        *[dma((2, ring))] * 2,
        *[dma((2, 3, ring))] * 4,
        *[dma((2, ring))] * 2,
        *[dma((n_groups,))] * 8,
    ]
    any_spec = pl.BlockSpec(memory_space=pl.ANY)
    shapes = (jax.ShapeDtypeStruct(cotangent.shape, BF16), jax.ShapeDtypeStruct(alpha.shape, BF16))
    results = pl.pallas_call(
        functools.partial(kernel, side, n_lev, blocks, slots, n_wide, width),
        out_shape=shapes,
        in_specs=[any_spec] * 8,
        out_specs=(any_spec, any_spec),
        scratch_shapes=scratch,
        compiler_params=pltpu.CompilerParams(
            collective_id=0, has_side_effects=True, vmem_limit_bytes=VMEM_LIMIT
        ),
    )(
        alpha, ens, htile, vloc.T, pattern.T,
        region_sizes.reshape(1, n_wide), owner.reshape(1, n_wide), cotangent,
    )
    whole = pl.BlockSpec(memory_space=pltpu.VMEM)
    return pl.pallas_call(
        hand_over,
        out_shape=shapes,
        in_specs=[whole] * 2,
        out_specs=(whole, whole),
        compiler_params=pltpu.CompilerParams(vmem_limit_bytes=VMEM_LIMIT),
    )(*results)


def solution(mesh):
    placed = (
        P("wide", None, "lev", None),
        P("wide", None, "lev", None),
        P(),
        P(),
        P(),
        P(),
        P(),
        P(None, "lev", "wide"),
    )
    return jax.shard_map(
        functools.partial(body, mesh.shape["wide"], mesh.shape["lev"]),
        mesh=mesh,
        in_specs=placed,
        out_specs=(P(None, "lev", "wide"), P("wide", None, "lev", None)),
        check_vma=False,
    )
```

```python
import functools
import math

import jax
import jax.numpy as jnp
from jax import lax
from jax.experimental import pallas as pl
from jax.experimental.pallas import tpu as pltpu
from jax.sharding import PartitionSpec as P

REACH = 4
MESH = pl.DeviceIdType.MESH
F32 = jnp.float32
BF16 = jnp.bfloat16
I32 = jnp.int32
GATHER_AFTER = 2
VMEM_LIMIT = 60 * 1024 * 1024


def iota(shape, dim):
    return lax.broadcasted_iota(I32, shape, dim)


def halves_of(fields):
    first = iota(fields[0].shape, 0) < 4
    low, high = [], []
    for a, b in (fields[0:2], fields[2:4]):
        low.append(jnp.where(first, a, pltpu.roll(b, 4, 0)))
        high.append(jnp.where(first, pltpu.roll(a, 4, 0), b))
    return jnp.concatenate(low + high, axis=0)


def kernel(
    side, n_lev, blocks, slots, members, width,
    alpha_h, ens_h, htile_h, vloc_h, pattern_h, sizes_h, owner_h, cot_h,
    inc_h, grad_h,
    alpha_v, ens_v, tile_v, vloc_v, pat_v, size_v, own_v, tab_v, tab_s, pat_s,
    a3, x, tiles_t, band_v, e1, e2, p3, h0, h1, r0, r1, q0, q1, q0f, q1f, t0, t1,
    g0, g1, snap, run, grad_v, inc_v,
    local_sem, out_sem, ag1_s, ag1_r, ag2_s, ag2_r, rs1_s, rs1_r, rs2_s, rs2_r, up_s, up_r, dn_s, dn_r,
    bup_s, bup_r, bdn_s, bdn_r,
):
    n_wide = side * side
    bits = side.bit_length() - 1
    w_me, l_me = lax.axis_index("wide"), lax.axis_index("lev")
    z_me, y_me = w_me // side, w_me % side
    upper, lower = lax.rem(l_me + 1, n_lev), lax.rem(l_me + n_lev - 1, n_lev)
    steps = sorted(range(1, side), key=lambda d: -min(d, side - d))
    order = sorted(range(side), key=lambda d: (min(d, side - d), d))
    place = {d: p for p, d in enumerate(order)}
    cuts = (0, 1, min(5, side), side)
    groups = [(g, a, b) for g, (a, b) in enumerate(zip(cuts, cuts[1:])) if a < b]

    def along_y(d):
        return lax.rem(y_me + d, side)

    def along_z(d):
        return lax.rem(z_me + d, side)

    def at_y(y):
        return (z_me * side + y, l_me)

    def at_z(z):
        return (z * side + y_me, l_me)

    def remote(src, dst, s, r, device):
        return pltpu.make_async_remote_copy(
            src_ref=src, dst_ref=dst, send_sem=s, recv_sem=r, device_id=device, device_id_type=MESH
        )

    with jax.named_scope("load_and_greet"):
        loads = [
            pltpu.make_async_copy(src, dst, local_sem.at[i])
            for i, (src, dst) in enumerate(
                (
                    (sizes_h, size_v), (owner_h, own_v), (pattern_h, pat_v),
                    (alpha_h, alpha_v), (htile_h, tile_v), (vloc_h, vloc_v), (ens_h, ens_v), (pattern_h, pat_s),
                )
            )
        ]
        own0 = pltpu.make_async_copy(cot_h.at[0:2], g0.at[z_me * side], local_sem.at[8])
        own1 = pltpu.make_async_copy(cot_h.at[2:4], g1.at[y_me * side], local_sem.at[9])
        own0.start()
        own1.start()
        barrier = pltpu.get_barrier_semaphore()
        friends = [at_y(along_y(d)) for d in steps] + [at_z(along_z(d)) for d in steps]
        friends += [(w_me, upper), (w_me, lower)]
        for friend in friends:
            pl.semaphore_signal(barrier, inc=1, device_id=friend, device_id_type=MESH)
        for load in loads:
            load.start()

    with jax.named_scope("cotangent_stage_1"):
        own0.wait()
        own1.wait()
        mine0, mine1 = g0.at[z_me * side], g1.at[y_me * side]
        pl.semaphore_wait(barrier, len(friends))
        ag1, ag2 = {}, []
        for d in steps:
            p = place[side - d]
            to0, to1 = g0.at[z_me * side + p], g1.at[y_me * side + p]
            ag1[p] = (
                remote(mine0, to0, ag1_s.at[0, d - 1], ag1_r.at[0, d - 1], at_y(along_y(d))),
                remote(mine1, to1, ag1_s.at[1, d - 1], ag1_r.at[1, d - 1], at_z(along_z(d))),
            )
            for copy in ag1[p]:
                copy.start()

        def forward(g, a, b):
            for p in range(max(a, 1), b):
                for copy in ag1[p]:
                    copy.wait_recv()
            at0, at1 = pl.ds(z_me * side + a, b - a), pl.ds(y_me * side + a, b - a)
            for d in steps:
                pair = (
                    remote(
                        mine0 if g == 0 else g0.at[at0],
                        g0.at[z_me * side] if g == 0 else g0.at[at0],
                        ag2_s.at[0, g, d - 1], ag2_r.at[0, g, d - 1], at_z(along_z(d)),
                    ),
                    remote(
                        mine1 if g == 0 else g1.at[at1],
                        g1.at[y_me * side] if g == 0 else g1.at[at1],
                        ag2_s.at[1, g, d - 1], ag2_r.at[1, g, d - 1], at_y(along_y(d)),
                    ),
                )
                for copy in pair:
                    copy.start()
                ag2.extend(pair)

        forward(*groups[0])

    lane16, lane32 = iota((16, 128), 1), iota((32, 128), 1)

    def block_lanes(b):
        return pl.ds(pl.multiple_of(b * 128, 128), 128)

    with jax.named_scope("spread"):
        loads[3].wait()
        loads[7].wait()

        def split_alpha(b, _):
            a = alpha_v[0, :, :, block_lanes(b)].astype(F32)
            a3[b] = halves_of([a[f] for f in range(4)]).astype(BF16)
            return 0

        lax.fori_loop(0, blocks, split_alpha, 0, unroll=8)
        loads[4].wait()
        stacked = tile_v[...].reshape(slots * 128, 128)
        group = min(8, blocks)
        n_groups = blocks // group
        halo1 = []
        for c in range(n_groups):

            def pick(i, _, c=c):
                b = c * group + i
                at = pl.ds(pl.multiple_of(b * 32, 32), 32)
                for k in range(slots):
                    x[at, k * 128 : (k + 1) * 128] = a3[pat_s[k, b]]
                return 0

            lax.fori_loop(0, group, pick, 0, unroll=8)
            part = jnp.dot(
                x[c * group * 32 : (c + 1) * group * 32, :], stacked, preferred_element_type=F32
            ).astype(BF16)
            for i in range(group):
                b = c * group + i
                e1[0:32, b * 128 : (b + 1) * 128] = part[i * 32 : (i + 1) * 32]
            at = pl.ds(c * group * 128, group * 128)
            sends = [
                remote(e1.at[0:16, at], e1.at[48:64, at], dn_s.at[c], dn_r.at[c], (w_me, lower)),
                remote(e1.at[16:32, at], e1.at[32:48, at], up_s.at[c], up_r.at[c], (w_me, upper)),
            ]
            for copy in sends:
                copy.start()
            halo1 += sends
            if c == min(GATHER_AFTER, n_groups - 1):
                for group_of in groups[1:2]:
                    forward(*group_of)

    with jax.named_scope("cotangent_stage_2"):
        for group_of in groups[2:]:
            forward(*group_of)

    with jax.named_scope("tables"):
        for load in loads[:3]:
            load.wait()
        square = (n_wide, n_wide)
        rows, cols = iota(square, 0), iota(square, 1)
        size_b = jnp.broadcast_to(size_v[...], square)
        own_b = jnp.broadcast_to(own_v[...], square)
        start_c = jnp.sum(jnp.where(cols < rows, size_b, 0), axis=1, keepdims=True)
        size_c = jnp.sum(jnp.where(cols == rows, size_b, 0), axis=1, keepdims=True)
        own_c = jnp.sum(jnp.where(cols == rows, own_b, 0), axis=1, keepdims=True)
        held = own_c == cols
        base = 3 * slots
        tab_v[base : base + 1, 0:n_wide] = jnp.sum(jnp.where(held, start_c, 0), axis=0, keepdims=True)
        tab_v[base + 1 : base + 2, 0:n_wide] = jnp.sum(jnp.where(held, size_c, 0), axis=0, keepdims=True)
        tab_v[base + 2 : base + 3, 0:n_wide] = jnp.sum(jnp.where(cols == rows, start_c, 0), axis=0, keepdims=True)
        tab_v[base + 3 : base + 4, 0:n_wide] = size_v[...]


        def near(d):
            return jnp.where(2 * d <= side, jnp.maximum(2 * d - 1, 0), 2 * (side - d))

        z_own, y_own = lax.shift_right_logical(own_v[...], bits), own_v[...] & (side - 1)
        tab_v[base + 4 : base + 5, 0:n_wide] = z_own * side + near((y_own - y_me) & (side - 1))
        tab_v[base + 6 : base + 7, 0:n_wide] = y_own * side + near((z_own - z_me) & (side - 1))
        ends = iota((n_wide, blocks), 1) * 128 + 127
        covered = jnp.sum(jnp.where(start_c + size_c <= ends, 1, 0), axis=0, keepdims=True)
        tab_v[base + 5 : base + 6, 0:blocks] = jnp.minimum(covered, n_wide - 1)
        here, there = iota((blocks, blocks), 0), iota((blocks, blocks), 1)
        for k in range(slots):
            row = pat_v[k : k + 1, :]
            col = jnp.sum(jnp.where(here == there, row, 0), axis=1, keepdims=True)
            tab_v[k : k + 1, 0:blocks] = row
            before = jnp.max(jnp.where((col == row) & (here < there), here, -1), axis=0, keepdims=True)
            tab_v[slots + k : slots + k + 1, 0:blocks] = jnp.where(before < 0, blocks, before)
            last = jnp.max(jnp.where(col == there, here, -1), axis=0, keepdims=True)
            tab_v[2 * slots + k : 2 * slots + k + 1, 0:blocks] = jnp.where(last < 0, blocks, last)
        to_s = pltpu.make_async_copy(tab_v, tab_s, local_sem.at[10])
        to_s.start()

    with jax.named_scope("bands"):
        loads[5].wait()
        first_level = l_me * 8
        top = n_lev * 8
        half = iota((8, width), 0) < 4

        def pairs_of(v):
            r = pltpu.roll(v, 4, 0)
            return jnp.where(half, v, r), jnp.where(half, r, v)

        band_v[...] = jnp.transpose(vloc_v[...])
        band = band_v[pl.ds(pl.multiple_of(first_level, 8), 8), :]
        lows, highs = pairs_of(band)
        _, before = pairs_of(band_v[pl.ds(pl.multiple_of(jnp.maximum(first_level - 8, 0), 8), 8), :])
        after, _ = pairs_of(band_v[pl.ds(pl.multiple_of(jnp.minimum(first_level + 8, top - 8), 8), 8), :])

        def source_level(k):
            g, q = k // 16, k % 4
            return jnp.where(g == 0, q, jnp.where(g == 1, q + 4, jnp.where(g == 2, q - 4, q + 8)))

        def banded(values, inside, offset):
            total = jnp.zeros(offset.shape, F32)
            for o in range(width):
                column = jnp.broadcast_to(values[:, o : o + 1], offset.shape)
                total = total + jnp.where(inside & (offset == o), column, 0.0)
            return total

        def in_two(w):
            top_part = w.astype(BF16)
            rest = (w - top_part.astype(F32)).astype(BF16)
            return jnp.concatenate([top_part, rest], axis=0)

        shape = (32, 64)
        r, k = iota(shape, 0), iota(shape, 1)
        level_out, level_in = r % 8, source_level(k)
        inside = (r // 8 == (k % 16) // 4) & (first_level + level_in >= 0) & (first_level + level_in < top)
        down = in_two(banded(jnp.concatenate([band] * 4, axis=0), inside, level_in - level_out + REACH))
        shape = (128, 128)
        k, r = iota(shape, 0), iota(shape, 1)
        level_out, level_in = r % 8, source_level(k)
        inside = (r // 8 == (k % 16) // 4) & (first_level + level_in >= 0) & (first_level + level_in < top)
        inside = inside & (k < 64) & (r < 32)
        rows_in = [lows, lows, highs, highs, before, before, after, after] + [jnp.zeros((8, width), F32)] * 8
        up = banded(jnp.concatenate(rows_in, axis=0), inside, level_out - level_in + REACH)
        up = in_two(jnp.transpose(up)[0:32, 0:64])
        to_s.wait()
        my_start = tab_s[base, w_me]
        my_size = tab_s[base + 1, w_me]
        my_off = my_start & 127

    with jax.named_scope("ensemble"):
        loads[6].wait()

        def ens_block(b):
            return ens_v[0, :, :, block_lanes(b)].astype(F32).reshape(32, 128)

        for k in range(slots):
            tiles_t[k * 128 : (k + 1) * 128, :] = jnp.transpose(tile_v[k].astype(F32)).astype(BF16)

    with jax.named_scope("mix_down"):
        wide_mix = min(4, blocks)
        mixes = group // wide_mix

        def down_step(i, _):
            at = pl.ds(pl.multiple_of(i * wide_mix * 128, wide_mix * 128), wide_mix * 128)
            both = jnp.dot(down, e1[:, at], preferred_element_type=F32)
            local = (both[:32] + both[32:]).astype(BF16).astype(F32)
            for j in range(wide_mix):
                b = i * wide_mix + j
                p3[b] = local[:, j * 128 : (j + 1) * 128] * ens_block(b)
            return 0

        for c in range(n_groups):
            for copy in halo1[2 * c : 2 * c + 2]:
                copy.wait_recv()
            lax.fori_loop(c * mixes, (c + 1) * mixes, down_step, 0, unroll=mixes)

    with jax.named_scope("member_sum_stage_1"):

        def share(w, rows):
            start = tab_s[base, w]
            blk = lax.shift_right_logical(start, 7)
            first, second = p3[blk, rows], p3[jnp.minimum(blk + 1, blocks - 1), rows]
            return jnp.where(lane16 >= (start & 127), first, second).astype(BF16)

        rs1 = {}
        for g, a, b in reversed(groups):

            def shares(i, _, a=a, b=b):
                for p in range(a, b):
                    h0[i * side + p] = share(i * side + along_y(order[p]), slice(0, 16))
                    h1[i * side + p] = share(along_z(order[p]) * side + i, slice(16, 32))
                return 0

            lax.fori_loop(0, side, shares, 0, unroll=2)
            rs1[g] = []
            for d in steps:
                z, y = along_z(d), along_y(d)
                at0, at1, to = pl.ds(z * side + a, b - a), pl.ds(y * side + a, b - a), pl.ds(a, b - a)
                rs1[g].append(
                    remote(h0.at[at0], r0.at[d - 1, to], rs1_s.at[0, g, d - 1], rs1_r.at[0, g, d - 1], at_z(z))
                )
                rs1[g].append(
                    remote(h1.at[at1], r1.at[d - 1, to], rs1_s.at[1, g, d - 1], rs1_r.at[1, g, d - 1], at_y(y))
                )
            for copy in rs1[g]:
                copy.start()

        rs2 = []

        def finish(g, a, b):
            for copy in rs1[g]:
                copy.wait_recv()
            for h, got, q, qf, me in ((h0, r0, q0, q0f, z_me), (h1, r1, q1, q1f, y_me)):
                for p in range(a, b):
                    total = h[me * side + p].astype(F32)
                    for d in range(side - 1):
                        total = total + got[d, p].astype(F32)
                    if p == 0:
                        qf[...] = total
                    else:
                        q[p] = total.astype(BF16)
            for p in reversed(range(max(a, 1), b)):
                d = order[p]
                pair = (
                    remote(q0.at[p], t0.at[d - 1], rs2_s.at[0, d - 1], rs2_r.at[0, d - 1], at_y(along_y(d))),
                    remote(q1.at[p], t1.at[d - 1], rs2_s.at[1, d - 1], rs2_r.at[1, d - 1], at_z(along_z(d))),
                )
                for copy in pair:
                    copy.start()
                rs2.extend(pair)

    with jax.named_scope("scaled"):
        for copy in ag2:
            copy.wait_recv()

        def paint(r, acc):
            start, size = tab_s[base + 2, r] & 127, tab_s[base + 3, r]
            first = g0[tab_s[base + 4, r]].astype(F32).reshape(16, 128)
            second = g1[tab_s[base + 6, r]].astype(F32).reshape(16, 128)
            tile = pltpu.roll(jnp.concatenate([first, second], axis=0), start, 1)
            acc = jnp.where((lane32 >= start) & (lane32 < start + size), tile, acc)
            snap[r] = acc
            return jnp.where(lane32 < start + size - 128, tile, acc)

        lax.fori_loop(0, n_wide, paint, jnp.zeros((32, 128), F32), unroll=8)
        for k in range(slots):
            run[k, blocks] = jnp.zeros((32, 128), F32)

        def link(b, _):
            s = ens_block(b) * snap[tab_s[base + 5, b]]
            s = halves_of([s[8 * f : 8 * f + 8] for f in range(4)]).astype(BF16).astype(F32)
            earlier = [run[k, tab_s[slots + k, b]] for k in range(slots)]
            for k in range(slots):
                run[k, b] = s + earlier[k]
            return 0

        lax.fori_loop(0, blocks, link, 0, unroll=4)

    with jax.named_scope("member_sum_far"):
        for group_of in groups[2:]:
            finish(*group_of)

    with jax.named_scope("tile_product"):
        halo2 = []
        for c in range(n_groups):

            def pick_back(i, _, c=c):
                j = c * group + i
                at = pl.ds(pl.multiple_of(j * 32, 32), 32)
                for k in range(slots):
                    x[at, k * 128 : (k + 1) * 128] = run[k, tab_s[2 * slots + k, j]].astype(BF16)
                return 0

            lax.fori_loop(0, group, pick_back, 0, unroll=8)
            part = jnp.dot(
                x[c * group * 32 : (c + 1) * group * 32, :], tiles_t[...], preferred_element_type=F32
            ).astype(BF16)
            for i in range(group):
                j = c * group + i
                e2[0:32, j * 128 : (j + 1) * 128] = part[i * 32 : (i + 1) * 32]
            at = pl.ds(c * group * 128, group * 128)
            sends = [
                remote(e2.at[0:16, at], e2.at[48:64, at], bdn_s.at[c], bdn_r.at[c], (w_me, lower)),
                remote(e2.at[16:32, at], e2.at[32:48, at], bup_s.at[c], bup_r.at[c], (w_me, upper)),
            ]
            for copy in sends:
                copy.start()
            halo2 += sends
            if c == max(n_groups - 2, 0):
                finish(*groups[1])

    with jax.named_scope("member_sum_stage_2"):
        finish(*groups[0])

    with jax.named_scope("mix_up"):
        outs = []

        def up_step(i, _):
            at = pl.ds(pl.multiple_of(i * wide_mix * 128, wide_mix * 128), wide_mix * 128)
            both = jnp.dot(up, e2[:, at], preferred_element_type=F32)
            local = (both[:32] + both[32:]).astype(BF16)
            for f in range(4):
                grad_v[f, :, at] = local[8 * f : 8 * f + 8]
            return 0

        for c in range(n_groups):
            for copy in halo2[2 * c : 2 * c + 2]:
                copy.wait_recv()
            lax.fori_loop(c * mixes, (c + 1) * mixes, up_step, 0, unroll=mixes)
            at = pl.ds(c * group * 128, group * 128)
            out = pltpu.make_async_copy(grad_v.at[:, :, at], grad_h.at[0, :, :, at], out_sem.at[c])
            out.start()
            outs.append(out)

    with jax.named_scope("increment"):
        for copy in rs2:
            copy.wait_recv()
        total0, total1 = q0f[...], q1f[...]
        for d in range(side - 1):
            total0 = total0 + t0[d].astype(F32)
            total1 = total1 + t1[d].astype(F32)
        total = jnp.concatenate([total0, total1], axis=0) * (1.0 / math.sqrt(members))
        total = pltpu.roll(total, (128 - my_off) & 127, 1)
        total = jnp.where(lane32 < my_size, total, 0.0)
        for f in range(4):
            inc_v[f] = total[8 * f : 8 * f + 8].astype(BF16)
        out = pltpu.make_async_copy(inc_v, inc_h, out_sem.at[n_groups])
        out.start()
        outs.append(out)

    with jax.named_scope("drain"):
        sent = [copy for pair in ag1.values() for copy in pair] + [copy for part in rs1.values() for copy in part]
        for copy in sent + ag2 + rs2 + halo1 + halo2:
            copy.wait_send()
        for out in outs:
            out.wait()


def hand_over(inc_h, grad_h, inc_out, grad_out, inc_v, grad_v, sem_in, sem_out):
    parts = [(grad_h.at[0, f], grad_v.at[f], grad_out.at[0, f]) for f in range(4)] + [(inc_h, inc_v, inc_out)]
    reads = [pltpu.make_async_copy(src, mid, sem_in.at[i]) for i, (src, mid, _) in enumerate(parts)]
    writes = [pltpu.make_async_copy(mid, dst, sem_out.at[i]) for i, (_, mid, dst) in enumerate(parts)]
    for read in reads:
        read.start()
    for read, write in zip(reads, writes):
        read.wait()
        write.start()
    for write in writes:
        write.wait()


def body(n_wide, n_lev, alpha, ens, htile, vloc, pattern, region_sizes, owner, cotangent):
    side = math.isqrt(n_wide)
    columns = alpha.shape[3]
    blocks = columns // 128
    slots = htile.shape[0]
    width = vloc.shape[1]
    group = min(8, blocks)
    n_groups = blocks // group
    dma = pltpu.SemaphoreType.DMA
    vmem = pltpu.VMEM
    ring = side - 1
    scratch = [
        vmem(alpha.shape, BF16), vmem(ens.shape, BF16), vmem(htile.shape, BF16), vmem(vloc.shape[::-1], F32),
        vmem(pattern.shape[::-1], I32), vmem((1, n_wide), I32), vmem((1, n_wide), I32),
        vmem((32, 128), I32), pltpu.SMEM((32, 128), I32),
        pltpu.SMEM(pattern.shape[::-1], I32),
        vmem((blocks, 32, 128), BF16),
        vmem((blocks * 32, slots * 128), BF16),
        vmem((slots * 128, 128), BF16),
        vmem(vloc.shape, F32),
        vmem((64, columns), BF16), vmem((64, columns), BF16),
        vmem((blocks, 32, 128), F32),
        vmem((n_wide, 16, 128), BF16), vmem((n_wide, 16, 128), BF16),
        vmem((ring, side, 16, 128), BF16), vmem((ring, side, 16, 128), BF16),
        vmem((side, 16, 128), BF16), vmem((side, 16, 128), BF16),
        vmem((16, 128), F32), vmem((16, 128), F32),
        vmem((ring, 16, 128), BF16), vmem((ring, 16, 128), BF16),
        vmem((n_wide, 2, 8, 128), BF16), vmem((n_wide, 2, 8, 128), BF16),
        vmem((n_wide, 32, 128), F32),
        vmem((slots, blocks + 1, 32, 128), F32),
        vmem(alpha.shape[1:], BF16), vmem(cotangent.shape, BF16),
        dma((11,)), dma((n_groups + 1,)),
        *[dma((2, ring))] * 2,
        *[dma((2, 3, ring))] * 4,
        *[dma((2, ring))] * 2,
        *[dma((n_groups,))] * 8,
    ]
    any_spec = pl.BlockSpec(memory_space=pl.ANY)
    shapes = (jax.ShapeDtypeStruct(cotangent.shape, BF16), jax.ShapeDtypeStruct(alpha.shape, BF16))
    results = pl.pallas_call(
        functools.partial(kernel, side, n_lev, blocks, slots, n_wide, width),
        out_shape=shapes,
        in_specs=[any_spec] * 8,
        out_specs=(any_spec, any_spec),
        scratch_shapes=scratch,
        compiler_params=pltpu.CompilerParams(
            collective_id=0, has_side_effects=True, vmem_limit_bytes=VMEM_LIMIT
        ),
    )(
        alpha, ens, htile, vloc.T, pattern.T,
        region_sizes.reshape(1, n_wide), owner.reshape(1, n_wide), cotangent,
    )
    return pl.pallas_call(
        hand_over,
        out_shape=shapes,
        in_specs=[any_spec] * 2,
        out_specs=(any_spec, any_spec),
        scratch_shapes=[vmem(cotangent.shape, BF16), vmem(alpha.shape[1:], BF16), dma((5,)), dma((5,))],
        compiler_params=pltpu.CompilerParams(vmem_limit_bytes=VMEM_LIMIT),
    )(*results)


def solution(mesh):
    placed = (
        P("wide", None, "lev", None),
        P("wide", None, "lev", None),
        P(),
        P(),
        P(),
        P(),
        P(),
        P(None, "lev", "wide"),
    )
    return jax.shard_map(
        functools.partial(body, mesh.shape["wide"], mesh.shape["lev"]),
        mesh=mesh,
        in_specs=placed,
        out_specs=(P(None, "lev", "wide"), P("wide", None, "lev", None)),
        check_vma=False,
    )
```

```python
import functools
import math

import jax
import jax.numpy as jnp
from jax import lax
from jax.experimental import pallas as pl
from jax.experimental.pallas import tpu as pltpu
from jax.sharding import PartitionSpec as P

REACH = 4
MESH = pl.DeviceIdType.MESH
F32 = jnp.float32
BF16 = jnp.bfloat16
I32 = jnp.int32
GATHER_AFTER = 2
VMEM_LIMIT = 60 * 1024 * 1024


def iota(shape, dim):
    return lax.broadcasted_iota(I32, shape, dim)


def halves_of(fields):
    first = iota(fields[0].shape, 0) < 4
    low, high = [], []
    for a, b in (fields[0:2], fields[2:4]):
        low.append(jnp.where(first, a, pltpu.roll(b, 4, 0)))
        high.append(jnp.where(first, pltpu.roll(a, 4, 0), b))
    return jnp.concatenate(low + high, axis=0)


def kernel(
    side, n_lev, blocks, slots, members, width,
    alpha_h, ens_h, htile_h, vloc_h, pattern_h, sizes_h, owner_h, cot_h,
    inc_h, grad_h,
    alpha_v, ens_v, tile_v, vloc_v, pat_v, size_v, own_v, tab_v, tab_s, pat_s,
    a3, x, tiles_t, band_v, e1, e2, p3, h0, h1, r0, r1, q0, q1, q0f, q1f, t0, t1,
    g0, g1, snap, run, grad_v, inc_v,
    local_sem, out_sem, ag1_s, ag1_r, ag2_s, ag2_r, rs1_s, rs1_r, rs2_s, rs2_r, up_s, up_r, dn_s, dn_r,
    bup_s, bup_r, bdn_s, bdn_r,
):
    n_wide = side * side
    bits = side.bit_length() - 1
    w_me, l_me = lax.axis_index("wide"), lax.axis_index("lev")
    z_me, y_me = w_me // side, w_me % side
    upper, lower = lax.rem(l_me + 1, n_lev), lax.rem(l_me + n_lev - 1, n_lev)
    steps = sorted(range(1, side), key=lambda d: -min(d, side - d))
    order = sorted(range(side), key=lambda d: (min(d, side - d), d))
    place = {d: p for p, d in enumerate(order)}
    cuts = (0, 1, min(5, side), side)
    groups = [(g, a, b) for g, (a, b) in enumerate(zip(cuts, cuts[1:])) if a < b]

    def along_y(d):
        return lax.rem(y_me + d, side)

    def along_z(d):
        return lax.rem(z_me + d, side)

    def at_y(y):
        return (z_me * side + y, l_me)

    def at_z(z):
        return (z * side + y_me, l_me)

    def remote(src, dst, s, r, device):
        return pltpu.make_async_remote_copy(
            src_ref=src, dst_ref=dst, send_sem=s, recv_sem=r, device_id=device, device_id_type=MESH
        )

    with jax.named_scope("load_and_greet"):
        loads = [
            pltpu.make_async_copy(src, dst, local_sem.at[i])
            for i, (src, dst) in enumerate(
                (
                    (sizes_h, size_v), (owner_h, own_v), (pattern_h, pat_v),
                    (alpha_h, alpha_v), (htile_h, tile_v), (vloc_h, vloc_v), (ens_h, ens_v), (pattern_h, pat_s),
                )
            )
        ]
        own0 = pltpu.make_async_copy(cot_h.at[0:2], g0.at[z_me * side], local_sem.at[8])
        own1 = pltpu.make_async_copy(cot_h.at[2:4], g1.at[y_me * side], local_sem.at[9])
        own0.start()
        own1.start()
        barrier = pltpu.get_barrier_semaphore()
        friends = [at_y(along_y(d)) for d in steps] + [at_z(along_z(d)) for d in steps]
        friends += [(w_me, upper), (w_me, lower)]
        for friend in friends:
            pl.semaphore_signal(barrier, inc=1, device_id=friend, device_id_type=MESH)
        for load in loads:
            load.start()

    with jax.named_scope("cotangent_stage_1"):
        own0.wait()
        own1.wait()
        mine0, mine1 = g0.at[z_me * side], g1.at[y_me * side]
        pl.semaphore_wait(barrier, len(friends))
        ag1, ag2 = {}, []
        for d in steps:
            p = place[side - d]
            to0, to1 = g0.at[z_me * side + p], g1.at[y_me * side + p]
            ag1[p] = (
                remote(mine0, to0, ag1_s.at[0, d - 1], ag1_r.at[0, d - 1], at_y(along_y(d))),
                remote(mine1, to1, ag1_s.at[1, d - 1], ag1_r.at[1, d - 1], at_z(along_z(d))),
            )
            for copy in ag1[p]:
                copy.start()

        def forward(g, a, b):
            for p in range(max(a, 1), b):
                for copy in ag1[p]:
                    copy.wait_recv()
            at0, at1 = pl.ds(z_me * side + a, b - a), pl.ds(y_me * side + a, b - a)
            for d in steps:
                pair = (
                    remote(
                        mine0 if g == 0 else g0.at[at0],
                        g0.at[z_me * side] if g == 0 else g0.at[at0],
                        ag2_s.at[0, g, d - 1], ag2_r.at[0, g, d - 1], at_z(along_z(d)),
                    ),
                    remote(
                        mine1 if g == 0 else g1.at[at1],
                        g1.at[y_me * side] if g == 0 else g1.at[at1],
                        ag2_s.at[1, g, d - 1], ag2_r.at[1, g, d - 1], at_y(along_y(d)),
                    ),
                )
                for copy in pair:
                    copy.start()
                ag2.extend(pair)


    lane16, lane32 = iota((16, 128), 1), iota((32, 128), 1)

    def block_lanes(b):
        return pl.ds(pl.multiple_of(b * 128, 128), 128)

    with jax.named_scope("spread"):
        loads[3].wait()
        loads[7].wait()

        def split_alpha(b, _):
            a = alpha_v[0, :, :, block_lanes(b)].astype(F32)
            a3[b] = halves_of([a[f] for f in range(4)]).astype(BF16)
            return 0

        lax.fori_loop(0, blocks, split_alpha, 0, unroll=8)
        loads[4].wait()
        stacked = tile_v[...].reshape(slots * 128, 128)
        group = min(8, blocks)
        n_groups = blocks // group
        halo1 = []
        for c in range(n_groups):

            def pick(i, _, c=c):
                b = c * group + i
                at = pl.ds(pl.multiple_of(b * 32, 32), 32)
                for k in range(slots):
                    x[at, k * 128 : (k + 1) * 128] = a3[pat_s[k, b]]
                return 0

            lax.fori_loop(0, group, pick, 0, unroll=8)
            part = jnp.dot(
                x[c * group * 32 : (c + 1) * group * 32, :], stacked, preferred_element_type=F32
            ).astype(BF16)
            for i in range(group):
                b = c * group + i
                e1[0:32, b * 128 : (b + 1) * 128] = part[i * 32 : (i + 1) * 32]
            at = pl.ds(c * group * 128, group * 128)
            sends = [
                remote(e1.at[0:16, at], e1.at[48:64, at], dn_s.at[c], dn_r.at[c], (w_me, lower)),
                remote(e1.at[16:32, at], e1.at[32:48, at], up_s.at[c], up_r.at[c], (w_me, upper)),
            ]
            for copy in sends:
                copy.start()
            halo1 += sends
            if c == 0:
                forward(*groups[0])
            if c == min(GATHER_AFTER, n_groups - 1):
                for group_of in groups[1:2]:
                    forward(*group_of)

    with jax.named_scope("cotangent_stage_2"):
        for group_of in groups[2:]:
            forward(*group_of)

    with jax.named_scope("tables"):
        for load in loads[:3]:
            load.wait()
        square = (n_wide, n_wide)
        rows, cols = iota(square, 0), iota(square, 1)
        size_b = jnp.broadcast_to(size_v[...], square)
        own_b = jnp.broadcast_to(own_v[...], square)
        start_c = jnp.sum(jnp.where(cols < rows, size_b, 0), axis=1, keepdims=True)
        size_c = jnp.sum(jnp.where(cols == rows, size_b, 0), axis=1, keepdims=True)
        own_c = jnp.sum(jnp.where(cols == rows, own_b, 0), axis=1, keepdims=True)
        held = own_c == cols
        base = 3 * slots
        tab_v[base : base + 1, 0:n_wide] = jnp.sum(jnp.where(held, start_c, 0), axis=0, keepdims=True)
        tab_v[base + 1 : base + 2, 0:n_wide] = jnp.sum(jnp.where(held, size_c, 0), axis=0, keepdims=True)
        tab_v[base + 2 : base + 3, 0:n_wide] = jnp.sum(jnp.where(cols == rows, start_c, 0), axis=0, keepdims=True)
        tab_v[base + 3 : base + 4, 0:n_wide] = size_v[...]


        def near(d):
            return jnp.where(2 * d <= side, jnp.maximum(2 * d - 1, 0), 2 * (side - d))

        z_own, y_own = lax.shift_right_logical(own_v[...], bits), own_v[...] & (side - 1)
        tab_v[base + 4 : base + 5, 0:n_wide] = z_own * side + near((y_own - y_me) & (side - 1))
        tab_v[base + 6 : base + 7, 0:n_wide] = y_own * side + near((z_own - z_me) & (side - 1))
        ends = iota((n_wide, blocks), 1) * 128 + 127
        covered = jnp.sum(jnp.where(start_c + size_c <= ends, 1, 0), axis=0, keepdims=True)
        tab_v[base + 5 : base + 6, 0:blocks] = jnp.minimum(covered, n_wide - 1)
        here, there = iota((blocks, blocks), 0), iota((blocks, blocks), 1)
        for k in range(slots):
            row = pat_v[k : k + 1, :]
            col = jnp.sum(jnp.where(here == there, row, 0), axis=1, keepdims=True)
            tab_v[k : k + 1, 0:blocks] = row
            before = jnp.max(jnp.where((col == row) & (here < there), here, -1), axis=0, keepdims=True)
            tab_v[slots + k : slots + k + 1, 0:blocks] = jnp.where(before < 0, blocks, before)
            last = jnp.max(jnp.where(col == there, here, -1), axis=0, keepdims=True)
            tab_v[2 * slots + k : 2 * slots + k + 1, 0:blocks] = jnp.where(last < 0, blocks, last)
        to_s = pltpu.make_async_copy(tab_v, tab_s, local_sem.at[10])
        to_s.start()

    with jax.named_scope("bands"):
        loads[5].wait()
        first_level = l_me * 8
        top = n_lev * 8
        half = iota((8, width), 0) < 4

        def pairs_of(v):
            r = pltpu.roll(v, 4, 0)
            return jnp.where(half, v, r), jnp.where(half, r, v)

        band_v[...] = jnp.transpose(vloc_v[...])
        band = band_v[pl.ds(pl.multiple_of(first_level, 8), 8), :]
        lows, highs = pairs_of(band)
        _, before = pairs_of(band_v[pl.ds(pl.multiple_of(jnp.maximum(first_level - 8, 0), 8), 8), :])
        after, _ = pairs_of(band_v[pl.ds(pl.multiple_of(jnp.minimum(first_level + 8, top - 8), 8), 8), :])

        def source_level(k):
            g, q = k // 16, k % 4
            return jnp.where(g == 0, q, jnp.where(g == 1, q + 4, jnp.where(g == 2, q - 4, q + 8)))

        def banded(values, inside, offset):
            total = jnp.zeros(offset.shape, F32)
            for o in range(width):
                column = jnp.broadcast_to(values[:, o : o + 1], offset.shape)
                total = total + jnp.where(inside & (offset == o), column, 0.0)
            return total

        def in_two(w):
            top_part = w.astype(BF16)
            rest = (w - top_part.astype(F32)).astype(BF16)
            return jnp.concatenate([top_part, rest], axis=0)

        shape = (32, 64)
        r, k = iota(shape, 0), iota(shape, 1)
        level_out, level_in = r % 8, source_level(k)
        inside = (r // 8 == (k % 16) // 4) & (first_level + level_in >= 0) & (first_level + level_in < top)
        down = in_two(banded(jnp.concatenate([band] * 4, axis=0), inside, level_in - level_out + REACH))
        shape = (128, 128)
        k, r = iota(shape, 0), iota(shape, 1)
        level_out, level_in = r % 8, source_level(k)
        inside = (r // 8 == (k % 16) // 4) & (first_level + level_in >= 0) & (first_level + level_in < top)
        inside = inside & (k < 64) & (r < 32)
        rows_in = [lows, lows, highs, highs, before, before, after, after] + [jnp.zeros((8, width), F32)] * 8
        up = banded(jnp.concatenate(rows_in, axis=0), inside, level_out - level_in + REACH)
        up = in_two(jnp.transpose(up)[0:32, 0:64])
        to_s.wait()
        my_start = tab_s[base, w_me]
        my_size = tab_s[base + 1, w_me]
        my_off = my_start & 127

    with jax.named_scope("ensemble"):
        loads[6].wait()

        def ens_block(b):
            return ens_v[0, :, :, block_lanes(b)].astype(F32).reshape(32, 128)

        for k in range(slots):
            tiles_t[k * 128 : (k + 1) * 128, :] = jnp.transpose(tile_v[k].astype(F32)).astype(BF16)

    with jax.named_scope("mix_down"):
        wide_mix = min(4, blocks)
        mixes = group // wide_mix

        def down_step(i, _):
            at = pl.ds(pl.multiple_of(i * wide_mix * 128, wide_mix * 128), wide_mix * 128)
            both = jnp.dot(down, e1[:, at], preferred_element_type=F32)
            local = (both[:32] + both[32:]).astype(BF16).astype(F32)
            for j in range(wide_mix):
                b = i * wide_mix + j
                p3[b] = local[:, j * 128 : (j + 1) * 128] * ens_block(b)
            return 0

        for c in range(n_groups):
            for copy in halo1[2 * c : 2 * c + 2]:
                copy.wait_recv()
            lax.fori_loop(c * mixes, (c + 1) * mixes, down_step, 0, unroll=mixes)

    with jax.named_scope("member_sum_stage_1"):

        def share(w, rows):
            start = tab_s[base, w]
            blk = lax.shift_right_logical(start, 7)
            first, second = p3[blk, rows], p3[jnp.minimum(blk + 1, blocks - 1), rows]
            return jnp.where(lane16 >= (start & 127), first, second).astype(BF16)

        rs1 = {}
        for g, a, b in reversed(groups):

            def shares(i, _, a=a, b=b):
                for p in range(a, b):
                    h0[i * side + p] = share(i * side + along_y(order[p]), slice(0, 16))
                    h1[i * side + p] = share(along_z(order[p]) * side + i, slice(16, 32))
                return 0

            lax.fori_loop(0, side, shares, 0, unroll=2)
            rs1[g] = []
            for d in steps:
                z, y = along_z(d), along_y(d)
                at0, at1, to = pl.ds(z * side + a, b - a), pl.ds(y * side + a, b - a), pl.ds(a, b - a)
                rs1[g].append(
                    remote(h0.at[at0], r0.at[d - 1, to], rs1_s.at[0, g, d - 1], rs1_r.at[0, g, d - 1], at_z(z))
                )
                rs1[g].append(
                    remote(h1.at[at1], r1.at[d - 1, to], rs1_s.at[1, g, d - 1], rs1_r.at[1, g, d - 1], at_y(y))
                )
            for copy in rs1[g]:
                copy.start()

        rs2 = []

        def finish(g, a, b):
            for copy in rs1[g]:
                copy.wait_recv()
            for h, got, q, qf, me in ((h0, r0, q0, q0f, z_me), (h1, r1, q1, q1f, y_me)):
                for p in range(a, b):
                    total = h[me * side + p].astype(F32)
                    for d in range(side - 1):
                        total = total + got[d, p].astype(F32)
                    if p == 0:
                        qf[...] = total
                    else:
                        q[p] = total.astype(BF16)
            for p in reversed(range(max(a, 1), b)):
                d = order[p]
                pair = (
                    remote(q0.at[p], t0.at[d - 1], rs2_s.at[0, d - 1], rs2_r.at[0, d - 1], at_y(along_y(d))),
                    remote(q1.at[p], t1.at[d - 1], rs2_s.at[1, d - 1], rs2_r.at[1, d - 1], at_z(along_z(d))),
                )
                for copy in pair:
                    copy.start()
                rs2.extend(pair)

    with jax.named_scope("scaled"):
        for copy in ag2:
            copy.wait_recv()

        def paint(r, acc):
            start, size = tab_s[base + 2, r] & 127, tab_s[base + 3, r]
            first = g0[tab_s[base + 4, r]].astype(F32).reshape(16, 128)
            second = g1[tab_s[base + 6, r]].astype(F32).reshape(16, 128)
            tile = pltpu.roll(jnp.concatenate([first, second], axis=0), start, 1)
            acc = jnp.where((lane32 >= start) & (lane32 < start + size), tile, acc)
            snap[r] = acc
            return jnp.where(lane32 < start + size - 128, tile, acc)

        lax.fori_loop(0, n_wide, paint, jnp.zeros((32, 128), F32), unroll=8)
        for k in range(slots):
            run[k, blocks] = jnp.zeros((32, 128), F32)

        def link(b, _):
            s = ens_block(b) * snap[tab_s[base + 5, b]]
            s = halves_of([s[8 * f : 8 * f + 8] for f in range(4)]).astype(BF16).astype(F32)
            earlier = [run[k, tab_s[slots + k, b]] for k in range(slots)]
            for k in range(slots):
                run[k, b] = s + earlier[k]
            return 0

        lax.fori_loop(0, blocks, link, 0, unroll=4)

    with jax.named_scope("tile_product"):
        halo2 = []
        for c in range(n_groups):

            def pick_back(i, _, c=c):
                j = c * group + i
                at = pl.ds(pl.multiple_of(j * 32, 32), 32)
                for k in range(slots):
                    x[at, k * 128 : (k + 1) * 128] = run[k, tab_s[2 * slots + k, j]].astype(BF16)
                return 0

            lax.fori_loop(0, group, pick_back, 0, unroll=8)
            part = jnp.dot(
                x[c * group * 32 : (c + 1) * group * 32, :], tiles_t[...], preferred_element_type=F32
            ).astype(BF16)
            for i in range(group):
                j = c * group + i
                e2[0:32, j * 128 : (j + 1) * 128] = part[i * 32 : (i + 1) * 32]
            at = pl.ds(c * group * 128, group * 128)
            sends = [
                remote(e2.at[0:16, at], e2.at[48:64, at], bdn_s.at[c], bdn_r.at[c], (w_me, lower)),
                remote(e2.at[16:32, at], e2.at[32:48, at], bup_s.at[c], bup_r.at[c], (w_me, upper)),
            ]
            for copy in sends:
                copy.start()
            halo2 += sends
            if c == 0:
                for group_of in groups[2:]:
                    finish(*group_of)
            if c == n_groups - 1:
                finish(*groups[1])

    with jax.named_scope("member_sum_stage_2"):
        finish(*groups[0])

    with jax.named_scope("mix_up"):
        outs = []

        def up_step(i, _):
            at = pl.ds(pl.multiple_of(i * wide_mix * 128, wide_mix * 128), wide_mix * 128)
            both = jnp.dot(up, e2[:, at], preferred_element_type=F32)
            local = (both[:32] + both[32:]).astype(BF16)
            for f in range(4):
                grad_v[f, :, at] = local[8 * f : 8 * f + 8]
            return 0

        for c in range(n_groups):
            for copy in halo2[2 * c : 2 * c + 2]:
                copy.wait_recv()
            lax.fori_loop(c * mixes, (c + 1) * mixes, up_step, 0, unroll=mixes)
            at = pl.ds(c * group * 128, group * 128)
            out = pltpu.make_async_copy(grad_v.at[:, :, at], grad_h.at[0, :, :, at], out_sem.at[c])
            out.start()
            outs.append(out)

    with jax.named_scope("increment"):
        for copy in rs2:
            copy.wait_recv()
        total0, total1 = q0f[...], q1f[...]
        for d in range(side - 1):
            total0 = total0 + t0[d].astype(F32)
            total1 = total1 + t1[d].astype(F32)
        total = jnp.concatenate([total0, total1], axis=0) * (1.0 / math.sqrt(members))
        total = pltpu.roll(total, (128 - my_off) & 127, 1)
        total = jnp.where(lane32 < my_size, total, 0.0)
        for f in range(4):
            inc_v[f] = total[8 * f : 8 * f + 8].astype(BF16)
        out = pltpu.make_async_copy(inc_v, inc_h, out_sem.at[n_groups])
        out.start()
        outs.append(out)

    with jax.named_scope("drain"):
        sent = [copy for pair in ag1.values() for copy in pair] + [copy for part in rs1.values() for copy in part]
        for copy in sent + ag2 + rs2 + halo1 + halo2:
            copy.wait_send()
        for out in outs:
            out.wait()


def hand_over(inc_h, grad_h, inc_out, grad_out, inc_v, grad_v, sem_in, sem_out):
    parts = [(grad_h.at[0, f], grad_v.at[f], grad_out.at[0, f]) for f in range(4)] + [(inc_h, inc_v, inc_out)]
    reads = [pltpu.make_async_copy(src, mid, sem_in.at[i]) for i, (src, mid, _) in enumerate(parts)]
    writes = [pltpu.make_async_copy(mid, dst, sem_out.at[i]) for i, (_, mid, dst) in enumerate(parts)]
    for read in reads:
        read.start()
    for read, write in zip(reads, writes):
        read.wait()
        write.start()
    for write in writes:
        write.wait()


def body(n_wide, n_lev, alpha, ens, htile, vloc, pattern, region_sizes, owner, cotangent):
    side = math.isqrt(n_wide)
    columns = alpha.shape[3]
    blocks = columns // 128
    slots = htile.shape[0]
    width = vloc.shape[1]
    group = min(8, blocks)
    n_groups = blocks // group
    dma = pltpu.SemaphoreType.DMA
    vmem = pltpu.VMEM
    ring = side - 1
    scratch = [
        vmem(alpha.shape, BF16), vmem(ens.shape, BF16), vmem(htile.shape, BF16), vmem(vloc.shape[::-1], F32),
        vmem(pattern.shape[::-1], I32), vmem((1, n_wide), I32), vmem((1, n_wide), I32),
        vmem((32, 128), I32), pltpu.SMEM((32, 128), I32),
        pltpu.SMEM(pattern.shape[::-1], I32),
        vmem((blocks, 32, 128), BF16),
        vmem((blocks * 32, slots * 128), BF16),
        vmem((slots * 128, 128), BF16),
        vmem(vloc.shape, F32),
        vmem((64, columns), BF16), vmem((64, columns), BF16),
        vmem((blocks, 32, 128), F32),
        vmem((n_wide, 16, 128), BF16), vmem((n_wide, 16, 128), BF16),
        vmem((ring, side, 16, 128), BF16), vmem((ring, side, 16, 128), BF16),
        vmem((side, 16, 128), BF16), vmem((side, 16, 128), BF16),
        vmem((16, 128), F32), vmem((16, 128), F32),
        vmem((ring, 16, 128), BF16), vmem((ring, 16, 128), BF16),
        vmem((n_wide, 2, 8, 128), BF16), vmem((n_wide, 2, 8, 128), BF16),
        vmem((n_wide, 32, 128), F32),
        vmem((slots, blocks + 1, 32, 128), F32),
        vmem(alpha.shape[1:], BF16), vmem(cotangent.shape, BF16),
        dma((11,)), dma((n_groups + 1,)),
        *[dma((2, ring))] * 2,
        *[dma((2, 3, ring))] * 4,
        *[dma((2, ring))] * 2,
        *[dma((n_groups,))] * 8,
    ]
    any_spec = pl.BlockSpec(memory_space=pl.ANY)
    shapes = (jax.ShapeDtypeStruct(cotangent.shape, BF16), jax.ShapeDtypeStruct(alpha.shape, BF16))
    results = pl.pallas_call(
        functools.partial(kernel, side, n_lev, blocks, slots, n_wide, width),
        out_shape=shapes,
        in_specs=[any_spec] * 8,
        out_specs=(any_spec, any_spec),
        scratch_shapes=scratch,
        compiler_params=pltpu.CompilerParams(
            collective_id=0, has_side_effects=True, vmem_limit_bytes=VMEM_LIMIT
        ),
    )(
        alpha, ens, htile, vloc.T, pattern.T,
        region_sizes.reshape(1, n_wide), owner.reshape(1, n_wide), cotangent,
    )
    return pl.pallas_call(
        hand_over,
        out_shape=shapes,
        in_specs=[any_spec] * 2,
        out_specs=(any_spec, any_spec),
        scratch_shapes=[vmem(cotangent.shape, BF16), vmem(alpha.shape[1:], BF16), dma((5,)), dma((5,))],
        compiler_params=pltpu.CompilerParams(vmem_limit_bytes=VMEM_LIMIT),
    )(*results)


def solution(mesh):
    placed = (
        P("wide", None, "lev", None),
        P("wide", None, "lev", None),
        P(),
        P(),
        P(),
        P(),
        P(),
        P(None, "lev", "wide"),
    )
    return jax.shard_map(
        functools.partial(body, mesh.shape["wide"], mesh.shape["lev"]),
        mesh=mesh,
        in_specs=placed,
        out_specs=(P(None, "lev", "wide"), P("wide", None, "lev", None)),
        check_vma=False,
    )
```

```python
import functools
import math

import jax
import jax.numpy as jnp
from jax import lax
from jax.experimental import pallas as pl
from jax.experimental.pallas import tpu as pltpu
from jax.sharding import PartitionSpec as P

REACH = 4
MESH = pl.DeviceIdType.MESH
F32 = jnp.float32
BF16 = jnp.bfloat16
I32 = jnp.int32
GATHER_AFTER = 2
VMEM_LIMIT = 60 * 1024 * 1024


def iota(shape, dim):
    return lax.broadcasted_iota(I32, shape, dim)


def halves_of(fields):
    first = iota(fields[0].shape, 0) < 4
    low, high = [], []
    for a, b in (fields[0:2], fields[2:4]):
        low.append(jnp.where(first, a, pltpu.roll(b, 4, 0)))
        high.append(jnp.where(first, pltpu.roll(a, 4, 0), b))
    return jnp.concatenate(low + high, axis=0)


def kernel(
    side, n_lev, blocks, slots, members, width,
    alpha_h, ens_h, htile_h, vloc_h, pattern_h, sizes_h, owner_h, cot_h,
    inc_h, grad_h,
    alpha_v, ens_v, tile_v, vloc_v, pat_v, size_v, own_v, tab_v, tab_s, pat_s,
    a3, x, tiles_t, band_v, e1, e2, p3, h0, h1, r0, r1, q0, q1, q0f, q1f, t0, t1,
    g0, g1, snap, run, grad_v, inc_v,
    local_sem, out_sem, ag1_s, ag1_r, ag2_s, ag2_r, rs1_s, rs1_r, rs2_s, rs2_r, up_s, up_r, dn_s, dn_r,
    bup_s, bup_r, bdn_s, bdn_r,
):
    n_wide = side * side
    bits = side.bit_length() - 1
    w_me, l_me = lax.axis_index("wide"), lax.axis_index("lev")
    z_me, y_me = w_me // side, w_me % side
    upper, lower = lax.rem(l_me + 1, n_lev), lax.rem(l_me + n_lev - 1, n_lev)
    steps = sorted(range(1, side), key=lambda d: -min(d, side - d))
    order = sorted(range(side), key=lambda d: (min(d, side - d), d))
    place = {d: p for p, d in enumerate(order)}
    cuts = (0, 1, min(5, side), side)
    groups = [(g, a, b) for g, (a, b) in enumerate(zip(cuts, cuts[1:])) if a < b]

    def along_y(d):
        return lax.rem(y_me + d, side)

    def along_z(d):
        return lax.rem(z_me + d, side)

    def at_y(y):
        return (z_me * side + y, l_me)

    def at_z(z):
        return (z * side + y_me, l_me)

    def remote(src, dst, s, r, device):
        return pltpu.make_async_remote_copy(
            src_ref=src, dst_ref=dst, send_sem=s, recv_sem=r, device_id=device, device_id_type=MESH
        )

    with jax.named_scope("load_and_greet"):
        loads = [
            pltpu.make_async_copy(src, dst, local_sem.at[i])
            for i, (src, dst) in enumerate(
                (
                    (sizes_h, size_v), (owner_h, own_v), (pattern_h, pat_v),
                    (alpha_h, alpha_v), (htile_h, tile_v), (vloc_h, vloc_v), (ens_h, ens_v), (pattern_h, pat_s),
                )
            )
        ]
        own0 = pltpu.make_async_copy(cot_h.at[0:2], g0.at[z_me * side], local_sem.at[8])
        own1 = pltpu.make_async_copy(cot_h.at[2:4], g1.at[y_me * side], local_sem.at[9])
        own0.start()
        own1.start()
        barrier = pltpu.get_barrier_semaphore()
        friends = [at_y(along_y(d)) for d in steps] + [at_z(along_z(d)) for d in steps]
        friends += [(w_me, upper), (w_me, lower)]
        for friend in friends:
            pl.semaphore_signal(barrier, inc=1, device_id=friend, device_id_type=MESH)
        for load in loads:
            load.start()

    with jax.named_scope("cotangent_stage_1"):
        own0.wait()
        own1.wait()
        mine0, mine1 = g0.at[z_me * side], g1.at[y_me * side]
        pl.semaphore_wait(barrier, len(friends))
        ag1, ag2 = {}, []
        for d in steps:
            p = place[side - d]
            to0, to1 = g0.at[z_me * side + p], g1.at[y_me * side + p]
            ag1[p] = (
                remote(mine0, to0, ag1_s.at[0, d - 1], ag1_r.at[0, d - 1], at_y(along_y(d))),
                remote(mine1, to1, ag1_s.at[1, d - 1], ag1_r.at[1, d - 1], at_z(along_z(d))),
            )
            for copy in ag1[p]:
                copy.start()

        def forward(g, a, b):
            for p in range(max(a, 1), b):
                for copy in ag1[p]:
                    copy.wait_recv()
            at0, at1 = pl.ds(z_me * side + a, b - a), pl.ds(y_me * side + a, b - a)
            for d in steps:
                pair = (
                    remote(
                        mine0 if g == 0 else g0.at[at0],
                        g0.at[z_me * side] if g == 0 else g0.at[at0],
                        ag2_s.at[0, g, d - 1], ag2_r.at[0, g, d - 1], at_z(along_z(d)),
                    ),
                    remote(
                        mine1 if g == 0 else g1.at[at1],
                        g1.at[y_me * side] if g == 0 else g1.at[at1],
                        ag2_s.at[1, g, d - 1], ag2_r.at[1, g, d - 1], at_y(along_y(d)),
                    ),
                )
                for copy in pair:
                    copy.start()
                ag2.extend(pair)


    lane16, lane32 = iota((16, 128), 1), iota((32, 128), 1)

    def block_lanes(b):
        return pl.ds(pl.multiple_of(b * 128, 128), 128)

    with jax.named_scope("spread"):
        loads[3].wait()
        loads[7].wait()

        def split_alpha(b, _):
            a = alpha_v[0, :, :, block_lanes(b)].astype(F32)
            a3[b] = halves_of([a[f] for f in range(4)]).astype(BF16)
            return 0

        lax.fori_loop(0, blocks, split_alpha, 0, unroll=8)
        loads[4].wait()
        stacked = tile_v[...].reshape(slots * 128, 128)
        group = min(8, blocks)
        n_groups = blocks // group
        halo1 = []
        for c in range(n_groups):

            def pick(i, _, c=c):
                b = c * group + i
                at = pl.ds(pl.multiple_of(b * 32, 32), 32)
                for k in range(slots):
                    x[at, k * 128 : (k + 1) * 128] = a3[pat_s[k, b]]
                return 0

            lax.fori_loop(0, group, pick, 0, unroll=8)
            part = jnp.dot(
                x[c * group * 32 : (c + 1) * group * 32, :], stacked, preferred_element_type=F32
            ).astype(BF16)
            for i in range(group):
                b = c * group + i
                e1[0:32, b * 128 : (b + 1) * 128] = part[i * 32 : (i + 1) * 32]
            at = pl.ds(c * group * 128, group * 128)
            sends = [
                remote(e1.at[0:16, at], e1.at[48:64, at], dn_s.at[c], dn_r.at[c], (w_me, lower)),
                remote(e1.at[16:32, at], e1.at[32:48, at], up_s.at[c], up_r.at[c], (w_me, upper)),
            ]
            for copy in sends:
                copy.start()
            halo1 += sends
            if c == 0:
                forward(*groups[0])
            if c == min(GATHER_AFTER, n_groups - 1):
                for group_of in groups[1:2]:
                    forward(*group_of)

    with jax.named_scope("cotangent_stage_2"):
        for group_of in groups[2:]:
            forward(*group_of)

    with jax.named_scope("tables"):
        for load in loads[:3]:
            load.wait()
        square = (n_wide, n_wide)
        rows, cols = iota(square, 0), iota(square, 1)
        size_b = jnp.broadcast_to(size_v[...], square)
        own_b = jnp.broadcast_to(own_v[...], square)
        start_c = jnp.sum(jnp.where(cols < rows, size_b, 0), axis=1, keepdims=True)
        size_c = jnp.sum(jnp.where(cols == rows, size_b, 0), axis=1, keepdims=True)
        own_c = jnp.sum(jnp.where(cols == rows, own_b, 0), axis=1, keepdims=True)
        held = own_c == cols
        base = 3 * slots
        tab_v[base : base + 1, 0:n_wide] = jnp.sum(jnp.where(held, start_c, 0), axis=0, keepdims=True)
        tab_v[base + 1 : base + 2, 0:n_wide] = jnp.sum(jnp.where(held, size_c, 0), axis=0, keepdims=True)
        tab_v[base + 2 : base + 3, 0:n_wide] = jnp.sum(jnp.where(cols == rows, start_c, 0), axis=0, keepdims=True)
        tab_v[base + 3 : base + 4, 0:n_wide] = size_v[...]


        def near(d):
            return jnp.where(2 * d <= side, jnp.maximum(2 * d - 1, 0), 2 * (side - d))

        z_own, y_own = lax.shift_right_logical(own_v[...], bits), own_v[...] & (side - 1)
        tab_v[base + 4 : base + 5, 0:n_wide] = z_own * side + near((y_own - y_me) & (side - 1))
        tab_v[base + 6 : base + 7, 0:n_wide] = y_own * side + near((z_own - z_me) & (side - 1))
        ends = iota((n_wide, blocks), 1) * 128 + 127
        covered = jnp.sum(jnp.where(start_c + size_c <= ends, 1, 0), axis=0, keepdims=True)
        tab_v[base + 5 : base + 6, 0:blocks] = jnp.minimum(covered, n_wide - 1)
        here, there = iota((blocks, blocks), 0), iota((blocks, blocks), 1)
        for k in range(slots):
            row = pat_v[k : k + 1, :]
            col = jnp.sum(jnp.where(here == there, row, 0), axis=1, keepdims=True)
            tab_v[k : k + 1, 0:blocks] = row
            before = jnp.max(jnp.where((col == row) & (here < there), here, -1), axis=0, keepdims=True)
            tab_v[slots + k : slots + k + 1, 0:blocks] = jnp.where(before < 0, blocks, before)
            last = jnp.max(jnp.where(col == there, here, -1), axis=0, keepdims=True)
            tab_v[2 * slots + k : 2 * slots + k + 1, 0:blocks] = jnp.where(last < 0, blocks, last)
        to_s = pltpu.make_async_copy(tab_v, tab_s, local_sem.at[10])
        to_s.start()

    with jax.named_scope("bands"):
        loads[5].wait()
        first_level = l_me * 8
        top = n_lev * 8
        half = iota((8, width), 0) < 4

        def pairs_of(v):
            r = pltpu.roll(v, 4, 0)
            return jnp.where(half, v, r), jnp.where(half, r, v)

        band_v[...] = jnp.transpose(vloc_v[...])
        band = band_v[pl.ds(pl.multiple_of(first_level, 8), 8), :]
        lows, highs = pairs_of(band)
        _, before = pairs_of(band_v[pl.ds(pl.multiple_of(jnp.maximum(first_level - 8, 0), 8), 8), :])
        after, _ = pairs_of(band_v[pl.ds(pl.multiple_of(jnp.minimum(first_level + 8, top - 8), 8), 8), :])

        def source_level(k):
            g, q = k // 16, k % 4
            return jnp.where(g == 0, q, jnp.where(g == 1, q + 4, jnp.where(g == 2, q - 4, q + 8)))

        def banded(values, inside, offset):
            total = jnp.zeros(offset.shape, F32)
            for o in range(width):
                column = jnp.broadcast_to(values[:, o : o + 1], offset.shape)
                total = total + jnp.where(inside & (offset == o), column, 0.0)
            return total

        def in_two(w):
            top_part = w.astype(BF16)
            rest = (w - top_part.astype(F32)).astype(BF16)
            return jnp.concatenate([top_part, rest], axis=0)

        shape = (32, 64)
        r, k = iota(shape, 0), iota(shape, 1)
        level_out, level_in = r % 8, source_level(k)
        inside = (r // 8 == (k % 16) // 4) & (first_level + level_in >= 0) & (first_level + level_in < top)
        down = in_two(banded(jnp.concatenate([band] * 4, axis=0), inside, level_in - level_out + REACH))
        shape = (128, 128)
        k, r = iota(shape, 0), iota(shape, 1)
        level_out, level_in = r % 8, source_level(k)
        inside = (r // 8 == (k % 16) // 4) & (first_level + level_in >= 0) & (first_level + level_in < top)
        inside = inside & (k < 64) & (r < 32)
        rows_in = [lows, lows, highs, highs, before, before, after, after] + [jnp.zeros((8, width), F32)] * 8
        up = banded(jnp.concatenate(rows_in, axis=0), inside, level_out - level_in + REACH)
        up = in_two(jnp.transpose(up)[0:32, 0:64])
        to_s.wait()
        my_start = tab_s[base, w_me]
        my_size = tab_s[base + 1, w_me]
        my_off = my_start & 127

    with jax.named_scope("ensemble"):
        loads[6].wait()

        def ens_block(b):
            return ens_v[0, :, :, block_lanes(b)].astype(F32).reshape(32, 128)

        for k in range(slots):
            tiles_t[k * 128 : (k + 1) * 128, :] = jnp.transpose(tile_v[k].astype(F32)).astype(BF16)

    with jax.named_scope("mix_down"):
        wide_mix = min(4, blocks)
        mixes = group // wide_mix

        def down_step(i, _):
            at = pl.ds(pl.multiple_of(i * wide_mix * 128, wide_mix * 128), wide_mix * 128)
            both = jnp.dot(down, e1[:, at], preferred_element_type=F32)
            local = (both[:32] + both[32:]).astype(BF16).astype(F32)
            for j in range(wide_mix):
                b = i * wide_mix + j
                p3[b] = local[:, j * 128 : (j + 1) * 128] * ens_block(b)
            return 0

        for c in range(n_groups):
            for copy in halo1[2 * c : 2 * c + 2]:
                copy.wait_recv()
            lax.fori_loop(c * mixes, (c + 1) * mixes, down_step, 0, unroll=mixes)

    with jax.named_scope("member_sum_stage_1"):

        def share(w, rows):
            start = tab_s[base, w]
            blk = lax.shift_right_logical(start, 7)
            first, second = p3[blk, rows], p3[jnp.minimum(blk + 1, blocks - 1), rows]
            return jnp.where(lane16 >= (start & 127), first, second).astype(BF16)

        rs1 = {}
        for g, a, b in reversed(groups):

            def shares(i, _, a=a, b=b):
                for p in range(a, b):
                    h0[i * side + p] = share(i * side + along_y(order[p]), slice(0, 16))
                    h1[i * side + p] = share(along_z(order[p]) * side + i, slice(16, 32))
                return 0

            lax.fori_loop(0, side, shares, 0, unroll=2)
            rs1[g] = []
            for d in steps:
                z, y = along_z(d), along_y(d)
                at0, at1, to = pl.ds(z * side + a, b - a), pl.ds(y * side + a, b - a), pl.ds(a, b - a)
                rs1[g].append(
                    remote(h0.at[at0], r0.at[d - 1, to], rs1_s.at[0, g, d - 1], rs1_r.at[0, g, d - 1], at_z(z))
                )
                rs1[g].append(
                    remote(h1.at[at1], r1.at[d - 1, to], rs1_s.at[1, g, d - 1], rs1_r.at[1, g, d - 1], at_y(y))
                )
            for copy in rs1[g]:
                copy.start()

        rs2 = []

        def finish(g, a, b):
            for copy in rs1[g]:
                copy.wait_recv()
            for h, got, q, qf, me in ((h0, r0, q0, q0f, z_me), (h1, r1, q1, q1f, y_me)):
                for p in range(a, b):
                    total = h[me * side + p].astype(F32)
                    for d in range(side - 1):
                        total = total + got[d, p].astype(F32)
                    if p == 0:
                        qf[...] = total
                    else:
                        q[p] = total.astype(BF16)
            for p in reversed(range(max(a, 1), b)):
                d = order[p]
                pair = (
                    remote(q0.at[p], t0.at[d - 1], rs2_s.at[0, d - 1], rs2_r.at[0, d - 1], at_y(along_y(d))),
                    remote(q1.at[p], t1.at[d - 1], rs2_s.at[1, d - 1], rs2_r.at[1, d - 1], at_z(along_z(d))),
                )
                for copy in pair:
                    copy.start()
                rs2.extend(pair)

    with jax.named_scope("scaled"):
        for copy in ag2:
            copy.wait_recv()

        def paint(r, acc):
            start, size = tab_s[base + 2, r] & 127, tab_s[base + 3, r]
            first = g0[tab_s[base + 4, r]].astype(F32).reshape(16, 128)
            second = g1[tab_s[base + 6, r]].astype(F32).reshape(16, 128)
            tile = pltpu.roll(jnp.concatenate([first, second], axis=0), start, 1)
            acc = jnp.where((lane32 >= start) & (lane32 < start + size), tile, acc)
            snap[r] = acc
            return jnp.where(lane32 < start + size - 128, tile, acc)

        lax.fori_loop(0, n_wide, paint, jnp.zeros((32, 128), F32), unroll=8)
        for k in range(slots):
            run[k, blocks] = jnp.zeros((32, 128), F32)

        def link(b, _):
            s = ens_block(b) * snap[tab_s[base + 5, b]]
            s = halves_of([s[8 * f : 8 * f + 8] for f in range(4)]).astype(BF16).astype(F32)
            earlier = [run[k, tab_s[slots + k, b]] for k in range(slots)]
            for k in range(slots):
                run[k, b] = s + earlier[k]
            return 0

        lax.fori_loop(0, blocks, link, 0, unroll=4)

    with jax.named_scope("member_sum_far"):
        for group_of in groups[2:]:
            finish(*group_of)

    with jax.named_scope("tile_product"):
        halo2 = []
        for c in range(n_groups):

            def pick_back(i, _, c=c):
                j = c * group + i
                at = pl.ds(pl.multiple_of(j * 32, 32), 32)
                for k in range(slots):
                    x[at, k * 128 : (k + 1) * 128] = run[k, tab_s[2 * slots + k, j]].astype(BF16)
                return 0

            lax.fori_loop(0, group, pick_back, 0, unroll=8)
            part = jnp.dot(
                x[c * group * 32 : (c + 1) * group * 32, :], tiles_t[...], preferred_element_type=F32
            ).astype(BF16)
            for i in range(group):
                j = c * group + i
                e2[0:32, j * 128 : (j + 1) * 128] = part[i * 32 : (i + 1) * 32]
            at = pl.ds(c * group * 128, group * 128)
            sends = [
                remote(e2.at[0:16, at], e2.at[48:64, at], bdn_s.at[c], bdn_r.at[c], (w_me, lower)),
                remote(e2.at[16:32, at], e2.at[32:48, at], bup_s.at[c], bup_r.at[c], (w_me, upper)),
            ]
            for copy in sends:
                copy.start()
            halo2 += sends
            if c == max(n_groups - 2, 0):
                finish(*groups[1])

    with jax.named_scope("member_sum_stage_2"):
        finish(*groups[0])

    with jax.named_scope("mix_up"):
        outs = []

        def up_step(i, _):
            at = pl.ds(pl.multiple_of(i * wide_mix * 128, wide_mix * 128), wide_mix * 128)
            both = jnp.dot(up, e2[:, at], preferred_element_type=F32)
            local = (both[:32] + both[32:]).astype(BF16)
            for f in range(4):
                grad_v[f, :, at] = local[8 * f : 8 * f + 8]
            return 0

        for c in range(n_groups):
            for copy in halo2[2 * c : 2 * c + 2]:
                copy.wait_recv()
            lax.fori_loop(c * mixes, (c + 1) * mixes, up_step, 0, unroll=mixes)
            at = pl.ds(c * group * 128, group * 128)
            out = pltpu.make_async_copy(grad_v.at[:, :, at], grad_h.at[0, :, :, at], out_sem.at[c])
            out.start()
            outs.append(out)

    with jax.named_scope("increment"):
        for copy in rs2:
            copy.wait_recv()
        total0, total1 = q0f[...], q1f[...]
        for d in range(side - 1):
            total0 = total0 + t0[d].astype(F32)
            total1 = total1 + t1[d].astype(F32)
        total = jnp.concatenate([total0, total1], axis=0) * (1.0 / math.sqrt(members))
        total = pltpu.roll(total, (128 - my_off) & 127, 1)
        total = jnp.where(lane32 < my_size, total, 0.0)
        for f in range(4):
            inc_v[f] = total[8 * f : 8 * f + 8].astype(BF16)
        out = pltpu.make_async_copy(inc_v, inc_h, out_sem.at[n_groups])
        out.start()
        outs.append(out)

    with jax.named_scope("drain"):
        sent = [copy for pair in ag1.values() for copy in pair] + [copy for part in rs1.values() for copy in part]
        for copy in sent + ag2 + rs2 + halo1 + halo2:
            copy.wait_send()
        for out in outs:
            out.wait()


def hand_over(inc_h, grad_h, inc_out, grad_out, inc_v, grad_v, sem_in, sem_out):
    parts = [(grad_h.at[0, f], grad_v.at[f], grad_out.at[0, f]) for f in range(4)] + [(inc_h, inc_v, inc_out)]
    reads = [pltpu.make_async_copy(src, mid, sem_in.at[i]) for i, (src, mid, _) in enumerate(parts)]
    writes = [pltpu.make_async_copy(mid, dst, sem_out.at[i]) for i, (_, mid, dst) in enumerate(parts)]
    for read in reads:
        read.start()
    for read, write in zip(reads, writes):
        read.wait()
        write.start()
    for write in writes:
        write.wait()


def body(n_wide, n_lev, alpha, ens, htile, vloc, pattern, region_sizes, owner, cotangent):
    side = math.isqrt(n_wide)
    columns = alpha.shape[3]
    blocks = columns // 128
    slots = htile.shape[0]
    width = vloc.shape[1]
    group = min(8, blocks)
    n_groups = blocks // group
    dma = pltpu.SemaphoreType.DMA
    vmem = pltpu.VMEM
    ring = side - 1
    scratch = [
        vmem(alpha.shape, BF16), vmem(ens.shape, BF16), vmem(htile.shape, BF16), vmem(vloc.shape[::-1], F32),
        vmem(pattern.shape[::-1], I32), vmem((1, n_wide), I32), vmem((1, n_wide), I32),
        vmem((32, 128), I32), pltpu.SMEM((32, 128), I32),
        pltpu.SMEM(pattern.shape[::-1], I32),
        vmem((blocks, 32, 128), BF16),
        vmem((blocks * 32, slots * 128), BF16),
        vmem((slots * 128, 128), BF16),
        vmem(vloc.shape, F32),
        vmem((64, columns), BF16), vmem((64, columns), BF16),
        vmem((blocks, 32, 128), F32),
        vmem((n_wide, 16, 128), BF16), vmem((n_wide, 16, 128), BF16),
        vmem((ring, side, 16, 128), BF16), vmem((ring, side, 16, 128), BF16),
        vmem((side, 16, 128), BF16), vmem((side, 16, 128), BF16),
        vmem((16, 128), F32), vmem((16, 128), F32),
        vmem((ring, 16, 128), BF16), vmem((ring, 16, 128), BF16),
        vmem((n_wide, 2, 8, 128), BF16), vmem((n_wide, 2, 8, 128), BF16),
        vmem((n_wide, 32, 128), F32),
        vmem((slots, blocks + 1, 32, 128), F32),
        vmem(alpha.shape[1:], BF16), vmem(cotangent.shape, BF16),
        dma((11,)), dma((n_groups + 1,)),
        *[dma((2, ring))] * 2,
        *[dma((2, 3, ring))] * 4,
        *[dma((2, ring))] * 2,
        *[dma((n_groups,))] * 8,
    ]
    any_spec = pl.BlockSpec(memory_space=pl.ANY)
    shapes = (jax.ShapeDtypeStruct(cotangent.shape, BF16), jax.ShapeDtypeStruct(alpha.shape, BF16))
    results = pl.pallas_call(
        functools.partial(kernel, side, n_lev, blocks, slots, n_wide, width),
        out_shape=shapes,
        in_specs=[any_spec] * 8,
        out_specs=(any_spec, any_spec),
        scratch_shapes=scratch,
        compiler_params=pltpu.CompilerParams(
            collective_id=0, has_side_effects=True, vmem_limit_bytes=VMEM_LIMIT
        ),
    )(
        alpha, ens, htile, vloc.T, pattern.T,
        region_sizes.reshape(1, n_wide), owner.reshape(1, n_wide), cotangent,
    )
    return pl.pallas_call(
        hand_over,
        out_shape=shapes,
        in_specs=[any_spec] * 2,
        out_specs=(any_spec, any_spec),
        scratch_shapes=[vmem(cotangent.shape, BF16), vmem(alpha.shape[1:], BF16), dma((5,)), dma((5,))],
        compiler_params=pltpu.CompilerParams(vmem_limit_bytes=VMEM_LIMIT),
    )(*results)


def solution(mesh):
    placed = (
        P("wide", None, "lev", None),
        P("wide", None, "lev", None),
        P(),
        P(),
        P(),
        P(),
        P(),
        P(None, "lev", "wide"),
    )
    return jax.shard_map(
        functools.partial(body, mesh.shape["wide"], mesh.shape["lev"]),
        mesh=mesh,
        in_specs=placed,
        out_specs=(P(None, "lev", "wide"), P("wide", None, "lev", None)),
        check_vma=False,
    )
```
